128 devices in a mesh: row: 16 (over x, y), col: 8 (over z, core).
Axes of the slice: x: 4, y: 4, z: 4, core: 2. Of those that a mesh axis runs over, the one named last changes fastest.
Arguments:
- features: bfloat16 [131072, 512], P(('row', 'col')), may hold values from -24 to 24
- weights: bfloat16 [1024, 512], replicated, may hold values from -0.25 to 0.25
- cotangent: bfloat16 [131072, 512], P(('row', 'col')), may hold values from -6 to 6
- neighbours: int32 [131072, 8], P(('row', 'col')), may hold values from 0 to 3071
- send_rows: int32 [128, 128, 8], P(('row', 'col')), may hold values from 0 to 1023
- send_count: int32 [128, 128], P(('row', 'col')), may hold values from 1 to 8, as said below
- hub_local: int32 [128, 8], P(('row', 'col')), may hold values from 0 to 1023
Outputs:
- activations: bfloat16 [131072, 512], P(('row', 'col'))
- grad_features: bfloat16 [131072, 512], P(('row', 'col'))
- grad_weights: float32 [1024, 512], P(('row', 'col'))
The draws below stay inside these ranges and needn't reach their ends.
Inputs may be any that keep to these rules, and one draw needn't show every extreme that they name: send_count[p, q] counts the live leading slots of send_rows[p, q]; in every draw some pair has 8 live slots, and some partition receives 8 live slots from every partition.
All inputs are finite; a program needn't handle non-finite values.
Results may differ from the reference program's by a relative error of at most 0.0051.
Values may be sent and summed in bfloat16 or wider, within the bound.
No kernel may reach another device: no remote copies, remote signals or barrier semaphores. Data moves between devices by JAX's collectives and lax.ppermute only.
A program may use at most 128 MiB of HBM per device.

```python
import jax
import jax.numpy as jnp
from jax import lax

D = 512
DEG = 8
NODE_DEV = 1024
HALO_PEER = 8
HUB_DEV = 8
PARTITIONS = 128
NODES = 131072
HUBS = 1024
TABLE = 3072


def draw_send_count(key, part):
    first, second, third = jax.random.split(jax.random.fold_in(key, 11), 3)
    base = jax.random.randint(first, (PARTITIONS, PARTITIONS), 1, HALO_PEER + 1)
    filled = jax.random.randint(second, (PARTITIONS, PARTITIONS), 0, 8) == 0
    column = jax.random.randint(third, (), 0, PARTITIONS)
    target = lax.broadcasted_iota(jnp.int32, (PARTITIONS, PARTITIONS), 1) == column
    return jnp.where(jnp.logical_or(filled, target), HALO_PEER, base).astype(jnp.int32)


def with_ends(array, rng, low, high):
    dims = array.shape
    index_at = [jax.random.randint(jax.random.fold_in(rng, axis), (), 0, dims[axis]) for axis in range(len(dims))]
    array = array.at[tuple(index_at)].set(low)
    longest = dims.index(max(dims))
    index_at[longest] = (index_at[longest] + 1) % dims[longest]
    return array.at[tuple(index_at)].set(high)


def raised(drawn, own_key, source, target, blocks, factor):
    owner, partner = [(jnp.arange(drawn.shape[position]) // (drawn.shape[position] // blocks)).reshape([-1 if axis == position else 1 for axis in range(drawn.ndim)]) for position in (source, target)]
    chosen = jax.random.permutation(own_key, blocks)[partner]
    strong = (owner == chosen) | (owner == (partner + blocks // 2) % blocks)
    return jnp.where(strong, factor * drawn, drawn)


def level_of(key, extent, shards, least, largest):
    gain = 1.0
    for axis_at, parts in shards:
        heights = jax.random.uniform(jax.random.fold_in(jax.random.fold_in(key, 6), axis_at), (parts,), jnp.float32, least / len(shards), largest / len(shards))
        gain = gain * jnp.repeat(jnp.exp(heights), extent[axis_at] // parts).reshape((-1,) + (1,) * (len(extent) - 1 - axis_at))
    return gain


def normal_values(key, dims, width, reach, pieces=(), kind=jnp.bfloat16):
    level = level_of(key, dims, pieces, -0.22, 0.18) if pieces else 1.0
    entries = jax.random.normal(key, dims, jnp.float32) * width * level
    return jnp.minimum(jnp.maximum(entries, -reach), reach).astype(kind)


def gaussian_with(own_key, dims, spread, bound, cuts, heavy, held_as=jnp.bfloat16):
    values = spread * jax.random.normal(own_key, dims, jnp.float32)
    if cuts:
        values = values * level_of(own_key, dims, cuts, -0.22, 0.18)
    return jnp.clip(raised(values, jax.random.fold_in(own_key, 3), *heavy), -bound, bound).astype(held_as)


def setup_inputs(seed: int = 0) -> dict:
    streams_of = jax.random.split(jax.random.key(seed), 8)
    features = gaussian_with(streams_of[0], (NODES, D), 1.0, 24.0, ((0, 128),), (0, 1, 128, 5.5))
    weights = normal_values(streams_of[1], (2 * D, D), D ** -0.5, 0.25)
    cotangent = normal_values(streams_of[2], (NODES, D), 1.0, 6.0, ((0, 128),))
    neighbours = with_ends(jax.random.randint(streams_of[3], (NODES, DEG), 0, TABLE), jax.random.fold_in(streams_of[3], 1), 0, TABLE - 1).astype(jnp.int32)
    send_rows = with_ends(jax.random.randint(streams_of[4], (PARTITIONS, PARTITIONS, HALO_PEER), 0, NODE_DEV), jax.random.fold_in(streams_of[4], 1), 0, NODE_DEV - 1).astype(jnp.int32)
    send_count = draw_send_count(jax.random.fold_in(streams_of[7], 71), 0)
    hub_local = with_ends(jax.random.randint(streams_of[6], (PARTITIONS, HUB_DEV), 0, NODE_DEV), jax.random.fold_in(streams_of[6], 1), 0, NODE_DEV - 1).astype(jnp.int32)
    return {"features": features, "weights": weights, "cotangent": cotangent, "neighbours": neighbours, "send_rows": send_rows, "send_count": send_count, "hub_local": hub_local}


def resolve(neighbours, send_rows, send_count, hub_local):
    owner_part = (jnp.arange(NODES, dtype=jnp.int32) // NODE_DEV)[:, None]
    halo_base = NODE_DEV
    hub_base = NODE_DEV + PARTITIONS * HALO_PEER
    halo_pos = jnp.clip(neighbours - halo_base, 0, PARTITIONS * HALO_PEER - 1)
    peer = halo_pos // HALO_PEER
    slot = halo_pos % HALO_PEER
    halo_node = peer * NODE_DEV + send_rows[peer, owner_part, slot]
    halo_live = slot < send_count[peer, owner_part]
    hub_pos = jnp.clip(neighbours - hub_base, 0, HUBS - 1)
    hub_owner = hub_pos // HUB_DEV
    hub_node = hub_owner * NODE_DEV + hub_local[hub_owner, hub_pos % HUB_DEV]
    is_own = neighbours < halo_base
    is_halo = jnp.logical_and(neighbours >= halo_base, neighbours < hub_base)
    source = jnp.where(is_own, owner_part * NODE_DEV + neighbours, jnp.where(is_halo, halo_node, hub_node))
    live = jnp.where(jnp.logical_and(is_halo, jnp.logical_not(halo_live)), 0.0, 1.0).astype(jnp.float32)
    return source.astype(jnp.int32), live


def reference(features, weights, cotangent, neighbours, send_rows, send_count, hub_local):
    source, live = resolve(neighbours, send_rows, send_count, hub_local)
    summed = jnp.zeros((NODES, D), jnp.float32)
    for slot_index in range(DEG):
        summed = summed + features[source[:, slot_index]].astype(jnp.float32) * live[:, slot_index:slot_index + 1]
    mean_rows = (summed / DEG).astype(jnp.bfloat16)
    pre = jnp.dot(features, weights[:D], preferred_element_type=jnp.float32)
    pre = pre + jnp.dot(mean_rows, weights[D:], preferred_element_type=jnp.float32)
    sigma = jax.nn.sigmoid(pre)
    activations = (pre * sigma).astype(jnp.bfloat16)
    delta = (cotangent.astype(jnp.float32) * sigma * (1.0 + pre * (1.0 - sigma))).astype(jnp.bfloat16)
    grad_weights = jnp.concatenate([
        jnp.dot(features.T, delta, preferred_element_type=jnp.float32),
        jnp.dot(mean_rows.T, delta, preferred_element_type=jnp.float32)], axis=0)
    grad_mean = jnp.dot(delta, weights[D:].T, preferred_element_type=jnp.float32) / DEG
    grad_rows = jnp.dot(delta, weights[:D].T, preferred_element_type=jnp.float32)
    for slot_index in range(DEG):
        grad_rows = grad_rows.at[source[:, slot_index]].add(grad_mean * live[:, slot_index:slot_index + 1])
    return activations, grad_rows.astype(jnp.bfloat16), grad_weights
```

```python
import jax
import jax.numpy as jnp
from jax import lax
from jax.experimental import pallas as pl
from jax.experimental.pallas import tpu as pltpu
from jax.sharding import PartitionSpec as P

BF = jnp.bfloat16
F32 = jnp.float32
DEG = 8
AXES = ("row", "col")
ROWS = 256
VM = pl.BlockSpec(memory_space=pltpu.VMEM)
SM = pl.BlockSpec(memory_space=pltpu.SMEM)
MIB = 1024 * 1024


def iota(shape, dim):
    return lax.broadcasted_iota(jnp.int32, shape, dim)


def mm(a, b):
    return jnp.dot(a, b, preferred_element_type=F32)


def mm_last(a, b):
    return lax.dot_general(a, b, (((1,), (1,)), ((), ())), preferred_element_type=F32)


def mm_first(a, b):
    return lax.dot_general(a, b, (((0,), (0,)), ((), ())), preferred_element_type=F32)


def params(mib):
    return pltpu.CompilerParams(vmem_limit_bytes=mib * MIB)


def send_kernel(f_ref, rows_ref, count_ref, hub_ref, out_ref, idx_ref):
    parts = rows_ref.shape[1]
    nodes = f_ref.shape[0]
    live = iota((8, parts), 0) < count_ref[...]
    idx = jnp.where(live, rows_ref[...], -1).astype(F32)
    idx_ref[...] = idx.T
    hub = jnp.broadcast_to(hub_ref[...], (8, 8))
    hub_col = jnp.sum(jnp.where(iota((8, 8), 0) == iota((8, 8), 1), hub, 0), axis=1, keepdims=True)
    hub_hot = (iota((8, nodes), 1) == hub_col).astype(F32).astype(BF)
    hub_rows = mm(hub_hot, f_ref[...])
    step = 16

    @pl.loop(0, parts // step)
    def _(b):
        blk = idx_ref[pl.ds(b * step, step), :]
        wide = jnp.broadcast_to(blk[:, None, :], (step, 8, 8)).reshape(step * 8, 8)
        pick = iota((step * 8, 8), 0) % 8 == iota((step * 8, 8), 1)
        col = jnp.sum(jnp.where(pick, wide, 0.0), axis=1, keepdims=True).astype(jnp.int32)
        hot = (iota((step * 8, nodes), 1) == col).astype(F32).astype(BF)
        listed = mm(hot, f_ref[...]).reshape(step, 8, -1)
        both = jnp.concatenate(
            [listed, jnp.broadcast_to(hub_rows[None], (step, 8, hub_rows.shape[1]))], axis=1
        )
        out_ref[pl.ds(b * step, step)] = both.astype(BF)


def hot_kernel(nb_ref, slot_ref, f_ref, w_ref, ar_ref, at_ref, st_ref, mown_ref, pre_ref, nbt_ref, ao_ref):
    nodes, width = f_ref.shape
    table = at_ref.shape[0]
    nb = nb_ref[...]
    w = nb - nodes
    is_hub = w >= (table - nodes) // 2
    v = jnp.where(is_hub, w - (table - nodes) // 2, w)
    v = nodes + (v // 8) * 16 + v % 8 + jnp.where(is_hub, 8, 0)
    t = jnp.where(nb < nodes, nb, v).astype(F32)
    nbt_ref[...] = t.T
    high = 32
    lanes = 256
    for c in range(nodes // lanes):
        rows = [jnp.broadcast_to(t[k : k + 1, c * lanes : (c + 1) * lanes], (high, lanes)) for k in range(DEG)]

        @pl.loop(0, table // high)
        def _(b):
            it = (iota((high, lanes), 0) + b * high).astype(F32)
            acc = jnp.where(it == rows[0], 1.0, 0.0)
            for k in range(1, DEG):
                acc = acc + jnp.where(it == rows[k], 1.0, 0.0)
            at_ref[pl.ds(b * high, high), c * lanes : (c + 1) * lanes] = acc.astype(BF)

    high = 16

    @pl.loop(0, nodes // high)
    def _(b):
        blk = nbt_ref[pl.ds(b * high, high), :]
        cols = [jnp.broadcast_to(blk[:, k : k + 1], (high, lanes)) for k in range(DEG)]
        base = iota((high, lanes), 1).astype(F32)
        for c in range(table // lanes):
            it = base + float(c * lanes)
            acc = jnp.where(it == cols[0], 1.0, 0.0)
            for k in range(1, DEG):
                acc = acc + jnp.where(it == cols[k], 1.0, 0.0)
            if c * lanes < nodes:
                ao_ref[pl.ds(b * high, high), c * lanes : (c + 1) * lanes] = acc.astype(BF)
            else:
                lo = c * lanes - nodes
                ar_ref[pl.ds(b * high, high), lo : lo + lanes] = acc.astype(BF)

    slot = slot_ref[...]

    @pl.loop(0, nodes // 16)
    def _(b):
        it = iota((16, slot.shape[1]), 0) + b * 16
        st_ref[pl.ds(b * 16, 16), :] = (it == slot).astype(F32).astype(BF)

    @pl.loop(0, nodes // ROWS)
    def _(b):
        r = pl.ds(b * ROWS, ROWS)
        mown_ref[r, :] = mm(ao_ref[r, :], f_ref[...])
        pre_ref[r, :] = mm(f_ref[r, :], w_ref[:width, :])


def mid_kernel(me_ref, recv_ref, ar_ref, at_ref, mown_ref, pre_ref, w_ref, f_ref, cot_ref,
               act_ref, delta_ref, gm_ref, pay_ref, gw_ref, mean_ref, acc_ref):
    nodes, width = delta_ref.shape
    w2 = w_ref[width:, :]

    @pl.loop(0, nodes // ROWS)
    def _(b):
        r = pl.ds(b * ROWS, ROWS)
        mean = ((mm(ar_ref[r, :], recv_ref[...]) + mown_ref[r, :]) / DEG).astype(BF)
        mean_ref[r, :] = mean
        pre = pre_ref[r, :] + mm(mean, w2)
        sig = jax.nn.sigmoid(pre)
        act_ref[r, :] = (pre * sig).astype(BF)
        delta = (cot_ref[r, :].astype(F32) * sig * (1.0 + pre * (1.0 - sig))).astype(BF)
        delta_ref[r, :] = delta
        gm_ref[r, :] = (mm_last(delta, w2) / DEG).astype(BF)

    own = nodes

    @pl.loop(0, pay_ref.shape[0] // ROWS)
    def _(b):
        r = pl.ds(b * ROWS, ROWS)
        pay_ref[r, :] = mm(at_ref[pl.ds(own + b * ROWS, ROWS), :], gm_ref[...]).astype(BF)

    me = me_ref[0]
    for half, x_ref in ((0, f_ref), (1, mean_ref)):
        for b in range(width // ROWS):
            part = mm_first(x_ref[:, b * ROWS : (b + 1) * ROWS], delta_ref[...])
            first = half * (width // 8) + b * (ROWS // 8)
            for j in range(ROWS // 8):
                at = pl.multiple_of(((first + j) ^ me) * 8, 8)
                acc_ref[pl.ds(at, 8), :] = part[j * 8 : (j + 1) * 8, :]
    gw_ref[...] = acc_ref[...].astype(BF)


def own_kernel(delta_ref, gm_ref, at_ref, w_ref, out_ref):
    nodes, width = delta_ref.shape

    @pl.loop(0, nodes // ROWS)
    def _(b):
        r = pl.ds(b * ROWS, ROWS)
        out_ref[r, :] = mm(at_ref[r, :], gm_ref[...]) + mm_last(delta_ref[r, :], w_ref[:width, :])


def last_kernel(st_ref, back_ref, own_ref, out_ref):
    @pl.loop(0, out_ref.shape[0] // ROWS)
    def _(b):
        r = pl.ds(b * ROWS, ROWS)
        out_ref[r, :] = (own_ref[r, :] + mm(st_ref[r, :], back_ref[...])).astype(BF)


def swap(x, bits, parts):
    return lax.ppermute(x, AXES, [(i, i ^ bits) for i in range(parts)])


def call(kernel, ins, outs, scratch=(), flops=0, read=0, mib=40, specs=None, exps=0):
    return pl.pallas_call(
        kernel,
        out_shape=[jax.ShapeDtypeStruct(s, d) for s, d in outs],
        in_specs=specs or [VM] * len(ins),
        out_specs=[VM] * len(outs),
        scratch_shapes=list(scratch),
        compiler_params=params(mib),
        cost_estimate=pl.CostEstimate(flops=flops, bytes_accessed=read, transcendentals=exps),
    )(*ins)


def local(features, weights, cotangent, neighbours, send_rows, send_count, hub_local):
    nodes, width = features.shape
    parts = lax.axis_size(AXES)
    recv_rows = parts * 16
    table = nodes + recv_rows
    me = lax.axis_index(AXES).astype(jnp.int32).reshape(1)

    (pay,) = call(
        send_kernel,
        [features, send_rows[0].T, send_count, hub_local],
        [((parts, 16, width), BF)],
        [pltpu.VMEM((parts, 8), F32)],
        flops=2 * nodes * parts * 8 * width, read=3 * MIB,
    )
    recv = lax.all_to_all(pay, AXES, split_axis=0, concat_axis=0, tiled=True).reshape(recv_rows, width)

    live = iota((parts, 8), 1) < send_count[0][:, None]
    slot = jnp.concatenate(
        [jnp.where(live, send_rows[0], -1), jnp.broadcast_to(hub_local, (parts, 8))], axis=1
    ).reshape(1, recv_rows)
    a_recv, a_t, s_t, mean_own, pre_own = call(
        hot_kernel,
        [neighbours.T, slot, features, weights],
        [((nodes, recv_rows), BF), ((table, nodes), BF), ((nodes, recv_rows), BF), ((nodes, width), F32), ((nodes, width), F32)],
        [pltpu.VMEM((nodes, DEG), F32), pltpu.VMEM((nodes, nodes), BF)],
        flops=14 * 10**9, read=20 * MIB,
    )
    act, delta, gm, back, gw = call(
        mid_kernel,
        [me, recv, a_recv, a_t, mean_own, pre_own, weights, features, cotangent],
        [((nodes, width), BF), ((nodes, width), BF), ((nodes, width), BF), ((recv_rows, width), BF), ((2 * width, width), BF)],
        [pltpu.VMEM((nodes, width), BF), pltpu.VMEM((2 * width, width), F32)],
        flops=8 * 10**9, read=20 * MIB,
        specs=[SM] + [VM] * 8,
    )
    back = lax.all_to_all(
        back.reshape(parts, 16, width), AXES, split_axis=0, concat_axis=0, tiled=True
    ).reshape(recv_rows, width)
    (own,) = call(own_kernel, [delta, gm, a_t, weights], [((nodes, width), F32)], flops=2 * 10**9, read=8 * MIB)

    blocks = gw.reshape(4, 4, 4, 2, 8, width)
    acc = blocks[:, :, :, 0].astype(F32) + swap(blocks[:, :, :, 1], 1, parts).astype(F32)
    for bits in (32, 8, 2):
        piece = acc.astype(BF)
        acc = acc[0] + sum(swap(piece[j], bits * j, parts).astype(F32) for j in (1, 2, 3))

    (grad,) = call(last_kernel, [s_t, back, own], [((nodes, width), BF)], flops=2 * 10**9, read=8 * MIB)
    return act, grad, acc.reshape(8, width)


def solution(mesh):
    both = P(AXES, None)
    placed = (both, P(), both, both, P(AXES, None, None), both, both)
    return jax.shard_map(local, mesh=mesh, in_specs=placed, out_specs=(both, both, both), check_vma=False)
```

```python
import jax
import jax.numpy as jnp
from jax import lax
from jax.experimental import pallas as pl
from jax.experimental.pallas import tpu as pltpu
from jax.sharding import PartitionSpec as P

BF = jnp.bfloat16
F32 = jnp.float32
DEG = 8
AXES = ("row", "col")
VM = pl.BlockSpec(memory_space=pltpu.VMEM)
SM = pl.BlockSpec(memory_space=pltpu.SMEM)
HB = pl.BlockSpec(memory_space=pltpu.HBM)
MIB = 1024 * 1024


def iota(shape, dim):
    return lax.broadcasted_iota(jnp.int32, shape, dim)


def mm(a, b):
    return jnp.dot(a, b, preferred_element_type=F32)


def mm_last(a, b):
    return lax.dot_general(a, b, (((1,), (1,)), ((), ())), preferred_element_type=F32)


def mm_first(a, b):
    return lax.dot_general(a, b, (((0,), (0,)), ((), ())), preferred_element_type=F32)


def send_kernel(f_hbm, rows_hbm, count_hbm, hub_hbm, out_hbm, f_ref, rows_ref, count_ref, hub_ref, idx_ref, out_ref, sem, out_sem):
    loads = [
        pltpu.make_async_copy(src, dst, sem.at[i])
        for i, (src, dst) in enumerate(
            ((f_hbm, f_ref), (rows_hbm, rows_ref), (count_hbm, count_ref), (hub_hbm, hub_ref))
        )
    ]
    for copy in loads:
        copy.start()
    for copy in loads[1:]:
        copy.wait()
    parts = rows_ref.shape[1]
    nodes = f_ref.shape[0]
    live = iota((8, parts), 0) < count_ref[...]
    idx = jnp.where(live, rows_ref[...], -1).astype(F32)
    idx_ref[...] = idx.T
    hub = jnp.broadcast_to(hub_ref[...], (8, 8))
    hub_col = jnp.sum(jnp.where(iota((8, 8), 0) == iota((8, 8), 1), hub, 0), axis=1, keepdims=True)
    hub_hot = (iota((8, nodes), 1) == hub_col).astype(F32).astype(BF)
    loads[0].wait()
    hub_rows = mm(hub_hot, f_ref[...])
    step = 32
    stores = []
    for b in range(parts // step):
        blk = idx_ref[b * step : (b + 1) * step, :]
        wide = jnp.broadcast_to(blk[:, None, :], (step, 8, 8)).reshape(step * 8, 8)
        pick = iota((step * 8, 8), 0) % 8 == iota((step * 8, 8), 1)
        col = jnp.sum(jnp.where(pick, wide, 0.0), axis=1, keepdims=True).astype(jnp.int32)
        hot = (iota((step * 8, nodes), 1) == col).astype(F32).astype(BF)
        listed = mm(hot, f_ref[...]).reshape(step, 8, -1)
        both = jnp.concatenate(
            [listed, jnp.broadcast_to(hub_rows[None], (step, 8, hub_rows.shape[1]))], axis=1
        )
        at = slice(b * step, (b + 1) * step)
        out_ref[at] = both.astype(BF)
        stores.append(pltpu.make_async_copy(out_ref.at[at], out_hbm.at[at], out_sem.at[b]))
        stores[-1].start()
    for copy in stores:
        copy.wait()


def unique(t):
    keep, count = [], []
    for k in range(DEG):
        row = t[k : k + 1]
        total = jnp.zeros_like(row)
        seen = None
        for j in range(DEG):
            same = t[j : j + 1] == row
            total = total + jnp.where(same, 1.0, 0.0)
            if j < k:
                seen = same if seen is None else seen | same
        keep.append(row if seen is None else jnp.where(seen, -1.0, row))
        count.append(total)
    return jnp.concatenate(keep, axis=0), jnp.concatenate(count, axis=0)


def count_matrix(u, m, out_ref):
    span, lanes = 256, 512
    nodes = u.shape[1]
    for c in range(nodes // lanes):
        at = slice(c * lanes, (c + 1) * lanes)
        counts = [jnp.broadcast_to(m[k : k + 1, at], (16, lanes)).astype(BF) for k in range(DEG)]
        base = iota((16, lanes), 0).astype(F32).astype(BF)

        @pl.loop(0, out_ref.shape[0] // span)
        def _(b):
            near = jnp.clip(u[:, at] - (b * span).astype(F32), -1.0, float(span))
            names = [jnp.broadcast_to(near[k : k + 1], (16, lanes)).astype(BF) for k in range(DEG)]
            for h in range(span // 16):
                it = base + BF(h * 16)
                acc = jnp.zeros((16, lanes), BF)
                for k in range(DEG):
                    acc = jnp.where(it == names[k], counts[k], acc)
                out_ref[pl.ds(pl.multiple_of(b * span + h * 16, 16), 16), at] = acc


def launch(pairs, sems, first=0):
    copies = [pltpu.make_async_copy(src, dst, sems.at[first + i]) for i, (src, dst) in enumerate(pairs)]
    for copy in copies:
        copy.start()
    return copies


def hot_kernel(nb_ref, slot_ref, f_ref, w_ref, at_hbm, mix_hbm, st_hbm, mown_hbm, pre_hbm,
               at_ref, mix_ref, st_ref, mown_ref, pre_ref, sems):
    nodes, width = f_ref.shape
    halo = mix_ref.shape[0] // 2
    u, m = unique(nb_ref[...].astype(F32))
    w = u.astype(jnp.int32) - nodes
    is_hub = w >= halo
    v = jnp.where(is_hub, w - halo, w)
    v = (v // 8) * 16 + v % 8 + jnp.where(is_hub, 8, 0)
    count_matrix(jnp.where(w < 0, -1, v).astype(F32), m, mix_ref)
    copies = launch([(mix_ref, mix_hbm)], sems, 0)
    count_matrix(u, m, at_ref)
    copies += launch([(at_ref, at_hbm)], sems, 1)
    mown_ref[...] = mm_first(at_ref[:nodes, :], f_ref[...])
    pre_ref[...] = mm(f_ref[...], w_ref[:width, :])
    copies += launch([(mown_ref, mown_hbm), (pre_ref, pre_hbm)], sems, 2)
    slot = slot_ref[...]

    @pl.loop(0, nodes // 16)
    def _(b):
        it = iota((16, slot.shape[1]), 0) + b * 16
        st_ref[pl.ds(pl.multiple_of(b * 16, 16), 16), :] = (it == slot).astype(F32).astype(BF)

    copies += launch([(st_ref, st_hbm)], sems, 4)
    for copy in copies:
        copy.wait()


def mid_kernel(core_ref, recv_hbm, mix_hbm, at_hbm, mown_hbm, pre_hbm, w_hbm, f_hbm, cot_hbm,
               act_hbm, delta_hbm, gm_hbm, give_hbm, keep_hbm,
               recv_ref, mix_ref, hub_ref, mown_ref, pre_ref, w2_ref, f_ref, cot_ref,
               act_ref, delta_ref, gm_ref, give_ref, keep_ref, mean_ref, in_sem, out_sem):
    nodes, width = delta_ref.shape
    step = 256
    steps = nodes // step
    rows = [slice(b * step, (b + 1) * step) for b in range(steps)]
    loads = launch(
        [(recv_hbm, recv_ref), (mix_hbm.at[:, rows[0]], mix_ref.at[:, rows[0]]), (w_hbm.at[width:, :], w2_ref)], in_sem, 0
    )
    blocks = []
    for b, r in enumerate(rows):
        pairs = [(x.at[r, :], y.at[r, :]) for x, y in ((mown_hbm, mown_ref), (pre_hbm, pre_ref), (cot_hbm, cot_ref))]
        if b:
            pairs.append((mix_hbm.at[:, r], mix_ref.at[:, r]))
        blocks.append(launch(pairs, in_sem, 3 + 4 * b))
    late = launch([(at_hbm.at[at_hbm.shape[0] - hub_ref.shape[0] :, :], hub_ref), (f_hbm, f_ref)], in_sem, 3 + 4 * steps)
    for copy in loads:
        copy.wait()
    stores = []
    for b, r in enumerate(rows):
        for copy in blocks[b]:
            copy.wait()
        mean = ((mm_first(mix_ref[:, r], recv_ref[...]) + mown_ref[r, :]) / DEG).astype(BF)
        mean_ref[r, :] = mean
        pre = pre_ref[r, :] + mm(mean, w2_ref[...])
        sig = jax.nn.sigmoid(pre)
        act_ref[r, :] = (pre * sig).astype(BF)
        delta = (cot_ref[r, :].astype(F32) * sig * (1.0 + pre * (1.0 - sig))).astype(BF)
        delta_ref[r, :] = delta
        gm_ref[r, :] = (mm_last(delta, w2_ref[...]) / DEG).astype(BF)
        stores += launch(
            [(x.at[r, :], y.at[r, :]) for x, y in ((act_ref, act_hbm), (delta_ref, delta_hbm), (gm_ref, gm_hbm))], out_sem, 3 * b
        )
    for copy in late:
        copy.wait()
    last = 3 * steps

    def fill(hub, weight):
        hub_ref_out, hub_hbm = hub
        weight_ref, weight_hbm = weight
        hub_ref_out[...] = mm(hub_ref[...], gm_ref[...]).astype(hub_ref_out.dtype)
        done = launch([(hub_ref_out, hub_hbm)], out_sem, last)
        for i, x in enumerate((f_ref, mean_ref)):
            r = slice(i * width, (i + 1) * width)
            weight_ref[r, :] = mm_first(x[...], delta_ref[...]).astype(weight_ref.dtype)
            done += launch([(weight_ref.at[r, :], weight_hbm.at[r, :])], out_sem, last + 1 + i)
        for copy in done:
            copy.wait()

    @pl.when(core_ref[0] == 0)
    def _():
        fill((keep_ref, keep_hbm), (give_ref, give_hbm))

    @pl.when(core_ref[0] != 0)
    def _():
        fill((give_ref, give_hbm), (keep_ref, keep_hbm))

    for copy in stores:
        copy.wait()


def own_kernel(delta_hbm, gm_hbm, at_hbm, w_hbm, own_hbm, halo_hbm,
               delta_ref, gm_ref, at_ref, w1_ref, own_ref, halo_ref, sems):
    nodes, width = delta_ref.shape
    rest = at_ref.shape[0]
    loads = launch(
        [
            (gm_hbm, gm_ref),
            (at_hbm.at[nodes:rest, :], at_ref.at[nodes:, :]),
            (at_hbm.at[:nodes, :], at_ref.at[:nodes, :]),
            (delta_hbm, delta_ref),
            (w_hbm.at[:width, :], w1_ref),
        ],
        sems,
    )
    loads[0].wait()
    loads[1].wait()
    halo_ref[...] = mm(at_ref[nodes:, :], gm_ref[...]).astype(BF)
    stores = launch([(halo_ref, halo_hbm)], sems, 5)
    for copy in loads[2:]:
        copy.wait()
    own_ref[...] = mm(at_ref[:nodes, :], gm_ref[...]) + mm_last(delta_ref[...], w1_ref[...])
    stores += launch([(own_ref, own_hbm)], sems, 6)
    for copy in stores:
        copy.wait()


def pack_kernel(halo_hbm, keep_hbm, got_hbm, out_hbm, halo_ref, keep_ref, got_ref, out_ref, in_sem, out_sem):
    parts = out_ref.shape[0]
    width = out_ref.shape[2]
    step = 32
    rows = [slice(b * step * 8, (b + 1) * step * 8) for b in range(parts // step)]
    loads = [
        launch([(x.at[r, :], y.at[r, :]) for x, y in ((halo_hbm, halo_ref), (keep_hbm, keep_ref), (got_hbm, got_ref))], in_sem, 3 * b)
        for b, r in enumerate(rows)
    ]
    stores = []
    for b, r in enumerate(rows):
        for copy in loads[b]:
            copy.wait()
        total = keep_ref[r, :] + got_ref[r, :].astype(F32)
        both = jnp.concatenate(
            [halo_ref[r, :].astype(F32).reshape(step, 8, width), total.reshape(step, 8, width)], axis=1
        )
        at = slice(b * step, (b + 1) * step)
        out_ref[at] = both.astype(BF)
        stores += launch([(out_ref.at[at], out_hbm.at[at])], out_sem, b)
    for copy in stores:
        copy.wait()


def last_kernel(st_ref, back_ref, own_ref, out_ref, weight_ref):
    out_ref[...] = (own_ref[...] + mm(st_ref[...], back_ref[...])).astype(BF)
    shape = (8, back_ref.shape[0])
    row = iota(shape, 1)
    odd = (row // 16) % 2 == 1
    take = jnp.where(odd & (row % 16 == iota(shape, 0) + 8), 1.0, 0.0).astype(BF)
    weight_ref[...] = mm(take, back_ref[...])


def call(kernel, ins, outs, scratch=(), flops=0, read=0, mib=60, in_specs=None, out_specs=None):
    return pl.pallas_call(
        kernel,
        out_shape=[jax.ShapeDtypeStruct(s, d) for s, d in outs],
        in_specs=in_specs or [HB] * len(ins),
        out_specs=out_specs or [HB] * len(outs),
        scratch_shapes=[pltpu.VMEM(*x) if isinstance(x, tuple) else x for x in scratch],
        compiler_params=pltpu.CompilerParams(vmem_limit_bytes=mib * MIB),
        cost_estimate=pl.CostEstimate(flops=flops, bytes_accessed=read, transcendentals=0),
    )(*ins)


def local(features, weights, cotangent, neighbours, send_rows, send_count, hub_local):
    nodes, width = features.shape
    parts = lax.axis_size(AXES)
    halo = parts * 8
    table = nodes + 2 * halo
    core = (lax.axis_index("col") % 2).astype(jnp.int32).reshape(1)
    sems = lambda n: pltpu.SemaphoreType.DMA((n,))
    wide, half = ((nodes, width), F32), ((nodes, width), BF)
    packed = ((parts, 16, width), BF)

    (pay,) = call(
        send_kernel,
        [features, send_rows[0].T, send_count, hub_local],
        [packed],
        [half, ((8, parts), jnp.int32), ((1, parts), jnp.int32), ((1, 8), jnp.int32), ((parts, 8), F32), packed, sems(4), sems(parts // 32)],
        flops=2 * nodes * halo * width, read=3 * MIB,
    )
    recv = lax.all_to_all(pay, AXES, split_axis=0, concat_axis=0, tiled=True).reshape(2 * halo, width)

    live = iota((parts, 8), 1) < send_count[0][:, None]
    even = iota((parts, 8), 0) % 2 == 0
    slot = jnp.concatenate(
        [jnp.where(live, send_rows[0], -1), jnp.where(even, hub_local, -1)], axis=1
    ).reshape(1, 2 * halo)
    hot = [((table, nodes), BF), ((2 * halo, nodes), BF), ((nodes, 2 * halo), BF), wide, wide]
    at, mix, st, mean_own, pre_own = call(
        hot_kernel, [neighbours.T, slot, features, weights], hot, hot + [sems(5)],
        flops=14 * 10**9, read=20 * MIB, in_specs=[VM] * 4,
    )
    mid = [half, half, half, ((2 * width, width), BF), ((2 * width, width), F32)]
    act, delta, gm, give, keep = call(
        mid_kernel,
        [core, recv, mix, at, mean_own, pre_own, weights, features, cotangent],
        mid,
        [((2 * halo, width), BF), ((2 * halo, nodes), BF), ((halo, nodes), BF), wide, wide, ((width, width), BF), half, half]
        + mid + [half, sems(21), sems(15)],
        flops=6 * 10**9, read=16 * MIB,
        in_specs=[SM] + [HB] * 8,
    )
    got = lax.ppermute(give, AXES, [(i, i ^ 1) for i in range(parts)])
    own_out = [wide, ((halo, width), BF)]
    own, halo_grad = call(
        own_kernel, [delta, gm, at, weights], own_out,
        [half, half, ((nodes + halo, nodes), BF), ((width, width), BF)] + own_out + [sems(7)],
        flops=3 * 10**9, read=8 * MIB,
    )
    (pay_back,) = call(
        pack_kernel, [halo_grad, keep, got], [packed],
        [((halo, width), BF), ((halo, width), F32), ((halo, width), BF), packed, sems(3 * parts // 32), sems(parts // 32)],
        flops=10**6, read=6 * MIB,
    )
    back = lax.all_to_all(pay_back, AXES, split_axis=0, concat_axis=0, tiled=True).reshape(2 * halo, width)
    grad, grad_weights = call(
        last_kernel, [st, back, own], [half, ((8, width), F32)], flops=2 * 10**9, read=8 * MIB, mib=16,
        in_specs=[VM] * 3, out_specs=[VM] * 2,
    )
    return act, grad, grad_weights


def solution(mesh):
    both = P(AXES, None)
    placed = (both, P(), both, both, P(AXES, None, None), both, both)
    return jax.shard_map(local, mesh=mesh, in_specs=placed, out_specs=(both, both, both), check_vma=False)
```

```python
import jax
import jax.numpy as jnp
from jax import lax
from jax.experimental import pallas as pl
from jax.experimental.pallas import tpu as pltpu
from jax.sharding import PartitionSpec as P

BF = jnp.bfloat16
F32 = jnp.float32
DEG = 8
AXES = ("row", "col")
VM = pl.BlockSpec(memory_space=pltpu.VMEM)
SM = pl.BlockSpec(memory_space=pltpu.SMEM)
HB = pl.BlockSpec(memory_space=pltpu.HBM)
MIB = 1024 * 1024


def iota(shape, dim):
    return lax.broadcasted_iota(jnp.int32, shape, dim)


def mm(a, b):
    return jnp.dot(a, b, preferred_element_type=F32)


def mm_last(a, b):
    return lax.dot_general(a, b, (((1,), (1,)), ((), ())), preferred_element_type=F32)


def mm_first(a, b):
    return lax.dot_general(a, b, (((0,), (0,)), ((), ())), preferred_element_type=F32)


def send_kernel(f_hbm, rows_hbm, count_hbm, hub_hbm, out_hbm, f_ref, rows_ref, count_ref, hub_ref, idx_ref, out_ref, sem, out_sem):
    loads = [
        pltpu.make_async_copy(src, dst, sem.at[i])
        for i, (src, dst) in enumerate(
            ((f_hbm, f_ref), (rows_hbm, rows_ref), (count_hbm, count_ref), (hub_hbm, hub_ref))
        )
    ]
    for copy in loads:
        copy.start()
    for copy in loads[1:]:
        copy.wait()
    parts = rows_ref.shape[1]
    nodes = f_ref.shape[0]
    live = iota((8, parts), 0) < count_ref[...]
    idx = jnp.where(live, rows_ref[...], -1).astype(F32)
    idx_ref[...] = idx.T
    hub = jnp.broadcast_to(hub_ref[...], (8, 8))
    hub_col = jnp.sum(jnp.where(iota((8, 8), 0) == iota((8, 8), 1), hub, 0), axis=1, keepdims=True)
    hub_hot = (iota((8, nodes), 1) == hub_col).astype(F32).astype(BF)
    loads[0].wait()
    hub_rows = mm(hub_hot, f_ref[...])
    step = 32
    stores = []
    for b in range(parts // step):
        blk = idx_ref[b * step : (b + 1) * step, :]
        wide = jnp.broadcast_to(blk[:, None, :], (step, 8, 8)).reshape(step * 8, 8)
        pick = iota((step * 8, 8), 0) % 8 == iota((step * 8, 8), 1)
        col = jnp.sum(jnp.where(pick, wide, 0.0), axis=1, keepdims=True).astype(jnp.int32)
        hot = (iota((step * 8, nodes), 1) == col).astype(F32).astype(BF)
        listed = mm(hot, f_ref[...]).reshape(step, 8, -1)
        both = jnp.concatenate(
            [listed, jnp.broadcast_to(hub_rows[None], (step, 8, hub_rows.shape[1]))], axis=1
        )
        at = slice(b * step, (b + 1) * step)
        out_ref[at] = both.astype(BF)
        stores.append(pltpu.make_async_copy(out_ref.at[at], out_hbm.at[at], out_sem.at[b]))
        stores[-1].start()
    for copy in stores:
        copy.wait()


def unique(t):
    keep, count = [], []
    for k in range(DEG):
        row = t[k : k + 1]
        total = jnp.zeros_like(row)
        seen = None
        for j in range(DEG):
            same = t[j : j + 1] == row
            total = total + jnp.where(same, 1.0, 0.0)
            if j < k:
                seen = same if seen is None else seen | same
        keep.append(row if seen is None else jnp.where(seen, -1.0, row))
        count.append(total)
    return jnp.concatenate(keep, axis=0), jnp.concatenate(count, axis=0)


def count_matrix(u, m, outs):
    span = 256
    first = 0
    for out_ref in outs:
        lanes = out_ref.shape[1]
        at = slice(first, first + lanes)
        first += lanes
        counts = [jnp.broadcast_to(m[k : k + 1, at], (16, lanes)).astype(BF) for k in range(DEG)]
        base = iota((16, lanes), 0).astype(F32).astype(BF)

        @pl.loop(0, out_ref.shape[0] // span)
        def _(b):
            near = jnp.clip(u[:, at] - (b * span).astype(F32), -1.0, float(span))
            names = [jnp.broadcast_to(near[k : k + 1], (16, lanes)).astype(BF) for k in range(DEG)]
            for h in range(0, span, 16):
                it = base + BF(h)
                acc = jnp.zeros((16, lanes), BF)
                for k in range(DEG):
                    acc = jnp.where(it == names[k], counts[k], acc)
                out_ref[pl.ds(pl.multiple_of(b * span + h, 16), 16), :] = acc


def launch(pairs, sems, first=0):
    copies = [pltpu.make_async_copy(src, dst, sems.at[first + i]) for i, (src, dst) in enumerate(pairs)]
    for copy in copies:
        copy.start()
    return copies


def hot_kernel(nb_ref, slot_ref, f_ref, own_hbm, listed_hbm, hub_hbm, mix_hbm, st_hbm, mown_hbm,
               own_ref, listed_ref, hub_ref, mix_ref, st_ref, mown_ref, sems):
    nodes = f_ref.shape[0]
    halo = hub_ref.shape[0]
    half = nodes // 2
    cols = [slice(0, half), slice(half, nodes)]
    u, m = unique(nb_ref[...].astype(F32))
    w = u.astype(jnp.int32) - nodes
    is_hub = w >= halo
    v = jnp.where(is_hub, w - halo, w)
    v = (v // 8) * 16 + v % 8 + jnp.where(is_hub, 8, 0)
    count_matrix(jnp.where(w < 0, -1, v).astype(F32), m, [mix_ref.at[c] for c in range(mix_ref.shape[0])])
    copies = launch([(mix_ref, mix_hbm)], sems, 0)
    count_matrix(u, m, [own_ref.at[:, c] for c in cols])
    mown_ref[...] = mm_first(own_ref[...], f_ref[...])
    copies += launch([(own_ref, own_hbm), (mown_ref, mown_hbm)], sems, 1)
    count_matrix(u - nodes, m, [listed_ref.at[:, c] for c in cols])
    count_matrix(u - (nodes + halo), m, [hub_ref.at[:, c] for c in cols])
    copies += launch([(listed_ref, listed_hbm), (hub_ref, hub_hbm)], sems, 3)
    slot = slot_ref[...]

    @pl.loop(0, nodes // 16)
    def _(b):
        it = iota((16, slot.shape[1]), 0) + b * 16
        st_ref[pl.ds(pl.multiple_of(b * 16, 16), 16), :] = (it == slot).astype(F32).astype(BF)

    copies += launch([(st_ref, st_hbm)], sems, 5)
    for copy in copies:
        copy.wait()


def mid_kernel(core_ref, recv_hbm, mix_hbm, at_hbm, mown_hbm, w_hbm, f_hbm, cot_hbm,
               act_hbm, delta_hbm, gm_hbm, mean_hbm, give_hbm,
               recv_ref, mix_ref, hub_ref, mown_ref, w_ref, f_ref, cot_ref, pre_ref,
               act_ref, delta_ref, gm_ref, mean_ref, give_ref, in_sem, out_sem):
    nodes, width = delta_ref.shape
    step = 256
    steps = nodes // step
    rows = [slice(b * step, (b + 1) * step) for b in range(steps)]
    early = launch([(w_hbm, w_ref), (f_hbm, f_ref)], in_sem, 0)
    loads = launch([(recv_hbm, recv_ref)], in_sem, 2)
    blocks = []
    for b, r in enumerate(rows):
        pairs = [(mix_hbm.at[b], mix_ref.at[b]), (mown_hbm.at[r, :], mown_ref.at[r, :]), (cot_hbm.at[r, :], cot_ref.at[r, :])]
        blocks.append(launch(pairs, in_sem, 3 + 3 * b))
    first = at_hbm.shape[0] - hub_ref.shape[0]
    hub_load = pltpu.make_async_copy(at_hbm.at[first:, :], hub_ref, in_sem.at[3 + 3 * steps])

    @pl.when(core_ref[0] != 0)
    def _():
        hub_load.start()

    for copy in early:
        copy.wait()
    pre_ref[...] = mm(f_ref[...], w_ref[:width, :])
    for copy in loads:
        copy.wait()
    w2 = w_ref[width:, :]
    stores = []
    for b, r in enumerate(rows):
        for copy in blocks[b]:
            copy.wait()
        mean = ((mm_first(mix_ref[b], recv_ref[...]) + mown_ref[r, :]) / DEG).astype(BF)
        mean_ref[r, :] = mean
        pre = pre_ref[r, :] + mm(mean, w2)
        sig = jax.nn.sigmoid(pre)
        act_ref[r, :] = (pre * sig).astype(BF)
        delta = (cot_ref[r, :].astype(F32) * sig * (1.0 + pre * (1.0 - sig))).astype(BF)
        delta_ref[r, :] = delta
        gm_ref[r, :] = (mm_last(delta, w2) / DEG).astype(BF)
        stores += launch(
            [(x.at[r, :], y.at[r, :]) for x, y in
             ((gm_ref, gm_hbm), (act_ref, act_hbm), (delta_ref, delta_hbm), (mean_ref, mean_hbm))],
            out_sem, 4 * b,
        )
    half = width
    tops = [slice(0, half), slice(half, 2 * half)]

    @pl.when(core_ref[0] == 0)
    def _():
        for i, (r, x) in enumerate(zip(tops, (f_ref, mean_ref))):
            give_ref[r, :] = mm_first(x[...], delta_ref[...]).astype(BF)
            pltpu.make_async_copy(give_ref.at[r, :], give_hbm.at[r, :], out_sem.at[4 * steps + i]).start()

    @pl.when(core_ref[0] != 0)
    def _():
        hub_load.wait()
        for i, r in enumerate(tops):
            give_ref[r, :] = mm(hub_ref[r, :], gm_ref[...]).astype(BF)
            pltpu.make_async_copy(give_ref.at[r, :], give_hbm.at[r, :], out_sem.at[4 * steps + i]).start()

    for i, r in enumerate(tops):
        pltpu.make_async_copy(give_ref.at[r, :], give_hbm.at[r, :], out_sem.at[4 * steps + i]).wait()
    for copy in stores:
        copy.wait()


def keep_kernel(core_ref, gm_hbm, at_hbm, f_hbm, mean_hbm, delta_hbm, keep_hbm,
                gm_ref, at_ref, f_ref, mean_ref, delta_ref, keep_ref, in_sem, out_sem):
    nodes, width = f_ref.shape
    halo = at_ref.shape[0]
    tops = [slice(0, width), slice(width, 2 * width)]

    @pl.when(core_ref[0] == 0)
    def _():
        first = at_hbm.shape[0] - halo
        loads = launch([(gm_hbm, gm_ref)] + [(at_hbm.at[first + r.start : first + r.stop, :], at_ref.at[r, :]) for r in tops], in_sem)
        loads[0].wait()
        stores = []
        for i, r in enumerate(tops):
            loads[1 + i].wait()
            keep_ref[r, :] = mm(at_ref[r, :], gm_ref[...])
            stores += launch([(keep_ref.at[r, :], keep_hbm.at[r, :])], out_sem, i)
        for copy in stores:
            copy.wait()

    @pl.when(core_ref[0] != 0)
    def _():
        loads = launch([(delta_hbm, delta_ref), (f_hbm, f_ref), (mean_hbm, mean_ref)], in_sem)
        loads[0].wait()
        stores = []
        for i, (r, x) in enumerate(zip(tops, (f_ref, mean_ref))):
            loads[1 + i].wait()
            keep_ref[r, :] = mm_first(x[...], delta_ref[...])
            stores += launch([(keep_ref.at[r, :], keep_hbm.at[r, :])], out_sem, i)
        for copy in stores:
            copy.wait()


def pack_kernel(gm_ref, at_ref, keep_hbm, got_ref, out_ref, keep_ref, sems):
    parts = out_ref.shape[0]
    width = out_ref.shape[2]
    step = 32
    rows = [slice(b * step * 8, (b + 1) * step * 8) for b in range(parts // step)]
    loads = launch([(keep_hbm.at[r, :], keep_ref.at[r, :]) for r in rows], sems)
    for b, r in enumerate(rows):
        listed = mm(at_ref[r, :], gm_ref[...])
        loads[b].wait()
        total = keep_ref[r, :] + got_ref[r, :].astype(F32)
        both = jnp.concatenate([listed.reshape(step, 8, width), total.reshape(step, 8, width)], axis=1)
        out_ref[b * step : (b + 1) * step] = both.astype(BF)


def last_kernel(st_ref, back_ref, at_ref, gm_ref, delta_ref, w_ref, out_hbm, weight_ref, out_ref, sems):
    width = out_ref.shape[1]
    step = 256
    shape = (8, back_ref.shape[0])
    row = iota(shape, 1)
    odd = (row // 16) % 2 == 1
    take = jnp.where(odd & (row % 16 == iota(shape, 0) + 8), 1.0, 0.0).astype(BF)
    weight_ref[...] = mm(take, back_ref[...])
    stores = []
    for b in range(out_ref.shape[0] // step):
        r = slice(b * step, (b + 1) * step)
        own = mm(at_ref[r, :], gm_ref[...]) + mm_last(delta_ref[r, :], w_ref[:width, :])
        out_ref[r, :] = (own + mm(st_ref[r, :], back_ref[...])).astype(BF)
        stores += launch([(out_ref.at[r, :], out_hbm.at[r, :])], sems, b)
    for copy in stores:
        copy.wait()


def call(kernel, ins, outs, scratch=(), flops=0, read=0, mib=60, in_specs=None, out_specs=None):
    return pl.pallas_call(
        kernel,
        out_shape=[jax.ShapeDtypeStruct(s, d) for s, d in outs],
        in_specs=in_specs or [HB] * len(ins),
        out_specs=out_specs or [HB] * len(outs),
        scratch_shapes=[pltpu.VMEM(*x) if isinstance(x, tuple) else x for x in scratch],
        compiler_params=pltpu.CompilerParams(vmem_limit_bytes=mib * MIB),
        cost_estimate=pl.CostEstimate(flops=flops, bytes_accessed=read, transcendentals=0),
    )(*ins)


def local(features, weights, cotangent, neighbours, send_rows, send_count, hub_local):
    nodes, width = features.shape
    parts = lax.axis_size(AXES)
    halo = parts * 8
    core = (lax.axis_index("col") % 2).astype(jnp.int32).reshape(1)
    sems = lambda n: pltpu.SemaphoreType.DMA((n,))
    wide, half = ((nodes, width), F32), ((nodes, width), BF)
    packed = ((parts, 16, width), BF)

    (pay,) = call(
        send_kernel,
        [features, send_rows[0].T, send_count, hub_local],
        [packed],
        [half, ((8, parts), jnp.int32), ((1, parts), jnp.int32), ((1, 8), jnp.int32), ((parts, 8), F32), packed, sems(4), sems(parts // 32)],
        flops=2 * nodes * halo * width, read=3 * MIB,
    )
    recv = lax.all_to_all(pay, AXES, split_axis=0, concat_axis=0, tiled=True).reshape(2 * halo, width)

    live = iota((parts, 8), 1) < send_count[0][:, None]
    even = iota((parts, 8), 0) % 2 == 0
    slot = jnp.concatenate(
        [jnp.where(live, send_rows[0], -1), jnp.where(even, hub_local, -1)], axis=1
    ).reshape(1, 2 * halo)
    square = ((nodes, nodes), BF)
    hot = [square, ((halo, nodes), BF), ((halo, nodes), BF), ((4, 2 * halo, nodes // 4), BF), ((nodes, 2 * halo), BF), wide]
    at_own, at_halo, at, mix, st, mean_own = call(
        hot_kernel, [neighbours.T, slot, features], hot, hot + [sems(6)],
        flops=14 * 10**9, read=20 * MIB, mib=63, in_specs=[VM] * 3,
    )
    both = ((2 * width, width), BF)
    mid = [half, half, half, half, both]
    act, delta, gm, mean, give = call(
        mid_kernel,
        [core, recv, mix, at, mean_own, weights, features, cotangent],
        mid,
        [((2 * halo, width), BF), ((4, 2 * halo, nodes // 4), BF), ((halo, nodes), BF), wide, both, half, half, wide]
        + mid + [sems(16), sems(18)],
        flops=6 * 10**9, read=16 * MIB, in_specs=[SM] + [HB] * 7,
    )
    got = lax.ppermute(give, AXES, [(i, i ^ 1) for i in range(parts)])
    (keep,) = call(
        keep_kernel, [core, gm, at, features, mean, delta], [((12 * halo, width), F32)],
        [half, ((halo, nodes), BF), half, half, half, ((halo, width), F32), sems(3), sems(2)],
        flops=2 * 10**9, read=8 * MIB, mib=56, in_specs=[SM] + [HB] * 5,
    )
    (pay_back,) = call(
        pack_kernel, [gm, at_halo, keep, got], [packed], [((halo, width), F32), sems(parts // 32)],
        flops=10**9, read=6 * MIB, mib=44, in_specs=[VM, VM, HB, VM], out_specs=[VM],
    )
    back = lax.all_to_all(pay_back, AXES, split_axis=0, concat_axis=0, tiled=True).reshape(2 * halo, width)
    grad, grad_weights = call(
        last_kernel, [st, back, at_own, gm, delta, weights], [half, ((8, width), F32)], [half, sems(4)],
        flops=4 * 10**9, read=10 * MIB, mib=24, in_specs=[VM] * 6, out_specs=[HB, VM],
    )
    return act, grad, grad_weights


def solution(mesh):
    both = P(AXES, None)
    placed = (both, P(), both, both, P(AXES, None, None), both, both)
    return jax.shard_map(local, mesh=mesh, in_specs=placed, out_specs=(both, both, both), check_vma=False)
```

```python
import jax
import jax.numpy as jnp
from jax import lax
from jax.experimental import pallas as pl
from jax.experimental.pallas import tpu as pltpu
from jax.sharding import PartitionSpec as P

BF = jnp.bfloat16
F32 = jnp.float32
DEG = 8
AXES = ("row", "col")
VM = pl.BlockSpec(memory_space=pltpu.VMEM)
SM = pl.BlockSpec(memory_space=pltpu.SMEM)
HB = pl.BlockSpec(memory_space=pltpu.HBM)
MIB = 1024 * 1024


def iota(shape, dim):
    return lax.broadcasted_iota(jnp.int32, shape, dim)


def mm(a, b):
    return jnp.dot(a, b, preferred_element_type=F32)


def mm_last(a, b):
    return lax.dot_general(a, b, (((1,), (1,)), ((), ())), preferred_element_type=F32)


def mm_first(a, b):
    return lax.dot_general(a, b, (((0,), (0,)), ((), ())), preferred_element_type=F32)


def send_kernel(f_hbm, rows_hbm, count_hbm, hub_hbm, out_hbm, f_ref, rows_ref, count_ref, hub_ref, idx_ref, out_ref, sem, out_sem):
    loads = [
        pltpu.make_async_copy(src, dst, sem.at[i])
        for i, (src, dst) in enumerate(
            ((f_hbm, f_ref), (rows_hbm, rows_ref), (count_hbm, count_ref), (hub_hbm, hub_ref))
        )
    ]
    for copy in loads:
        copy.start()
    for copy in loads[1:]:
        copy.wait()
    parts = rows_ref.shape[1]
    nodes = f_ref.shape[0]
    live = iota((8, parts), 0) < count_ref[...]
    idx = jnp.where(live, rows_ref[...], -1).astype(F32)
    idx_ref[...] = idx.T
    hub = jnp.broadcast_to(hub_ref[...], (8, 8))
    hub_col = jnp.sum(jnp.where(iota((8, 8), 0) == iota((8, 8), 1), hub, 0), axis=1, keepdims=True)
    hub_hot = (iota((8, nodes), 1) == hub_col).astype(F32).astype(BF)
    loads[0].wait()
    hub_rows = mm(hub_hot, f_ref[...])
    step = 32
    stores = []
    for b in range(parts // step):
        blk = idx_ref[b * step : (b + 1) * step, :]
        wide = jnp.broadcast_to(blk[:, None, :], (step, 8, 8)).reshape(step * 8, 8)
        pick = iota((step * 8, 8), 0) % 8 == iota((step * 8, 8), 1)
        col = jnp.sum(jnp.where(pick, wide, 0.0), axis=1, keepdims=True).astype(jnp.int32)
        hot = (iota((step * 8, nodes), 1) == col).astype(F32).astype(BF)
        listed = mm(hot, f_ref[...]).reshape(step, 8, -1)
        both = jnp.concatenate(
            [listed, jnp.broadcast_to(hub_rows[None], (step, 8, hub_rows.shape[1]))], axis=1
        )
        at = slice(b * step, (b + 1) * step)
        out_ref[at] = both.astype(BF)
        stores.append(pltpu.make_async_copy(out_ref.at[at], out_hbm.at[at], out_sem.at[b]))
        stores[-1].start()
    for copy in stores:
        copy.wait()


def unique(t):
    keep, count = [], []
    for k in range(DEG):
        row = t[k : k + 1]
        total = jnp.zeros_like(row)
        seen = None
        for j in range(DEG):
            same = t[j : j + 1] == row
            total = total + jnp.where(same, 1.0, 0.0)
            if j < k:
                seen = same if seen is None else seen | same
        keep.append(row if seen is None else jnp.where(seen, -1.0, row))
        count.append(total)
    return jnp.concatenate(keep, axis=0), jnp.concatenate(count, axis=0)


def count_matrix(u, m, outs):
    span = 256
    first = 0
    for out_ref in outs:
        lanes = out_ref.shape[1]
        at = slice(first, first + lanes)
        first += lanes
        counts = [jnp.broadcast_to(m[k : k + 1, at], (16, lanes)).astype(BF) for k in range(DEG)]
        base = iota((16, lanes), 0).astype(F32).astype(BF)

        @pl.loop(0, out_ref.shape[0] // span)
        def _(b):
            near = jnp.clip(u[:, at] - (b * span).astype(F32), -1.0, float(span))
            names = [jnp.broadcast_to(near[k : k + 1], (16, lanes)).astype(BF) for k in range(DEG)]
            for h in range(0, span, 16):
                it = base + BF(h)
                acc = jnp.zeros((16, lanes), BF)
                for k in range(DEG):
                    acc = jnp.where(it == names[k], counts[k], acc)
                out_ref[pl.ds(pl.multiple_of(b * span + h, 16), 16), :] = acc


def launch(pairs, sems, first=0):
    copies = [pltpu.make_async_copy(src, dst, sems.at[first + i]) for i, (src, dst) in enumerate(pairs)]
    for copy in copies:
        copy.start()
    return copies


def hot_kernel(nb_ref, slot_ref, f_ref, own_hbm, listed_hbm, hub_hbm, mix_hbm, st_hbm, mown_hbm,
               own_ref, listed_ref, hub_ref, mix_ref, st_ref, mown_ref, sems):
    nodes = f_ref.shape[0]
    halo = hub_ref.shape[0]
    half = nodes // 2
    cols = [slice(0, half), slice(half, nodes)]
    u, m = unique(nb_ref[...].astype(F32))
    w = u.astype(jnp.int32) - nodes
    is_hub = w >= halo
    v = jnp.where(is_hub, w - halo, w)
    v = (v // 8) * 16 + v % 8 + jnp.where(is_hub, 8, 0)
    count_matrix(jnp.where(w < 0, -1, v).astype(F32), m, [mix_ref.at[c] for c in range(mix_ref.shape[0])])
    copies = launch([(mix_ref, mix_hbm)], sems, 0)
    count_matrix(u, m, [own_ref.at[:, c] for c in cols])
    mown_ref[...] = mm_first(own_ref[...], f_ref[...])
    copies += launch([(own_ref, own_hbm), (mown_ref, mown_hbm)], sems, 1)
    count_matrix(u - nodes, m, [listed_ref.at[:, c] for c in cols])
    count_matrix(u - (nodes + halo), m, [hub_ref.at[:, c] for c in cols])
    copies += launch([(listed_ref, listed_hbm), (hub_ref, hub_hbm)], sems, 3)
    slot = slot_ref[...]

    @pl.loop(0, nodes // 16)
    def _(b):
        it = iota((16, slot.shape[1]), 0) + b * 16
        st_ref[pl.ds(pl.multiple_of(b * 16, 16), 16), :] = (it == slot).astype(F32).astype(BF)

    copies += launch([(st_ref, st_hbm)], sems, 5)
    for copy in copies:
        copy.wait()


def mid_kernel(core_ref, recv_hbm, mix_hbm, at_hbm, mown_hbm, w_hbm, f_hbm, cot_hbm,
               act_hbm, delta_hbm, gm_hbm, mean_hbm, give_hbm,
               recv_ref, mix_ref, hub_ref, mown_ref, w_ref, f_ref, cot_ref, pre_ref,
               act_ref, delta_ref, gm_ref, mean_ref, give_ref, in_sem, out_sem):
    nodes, width = delta_ref.shape
    step = 512
    steps = nodes // step
    rows = [slice(b * step, (b + 1) * step) for b in range(steps)]
    early = launch([(w_hbm, w_ref), (f_hbm, f_ref)], in_sem, 0)
    loads = launch([(recv_hbm, recv_ref)], in_sem, 2)
    blocks = []
    for b, r in enumerate(rows):
        pairs = [(mix_hbm.at[b], mix_ref.at[b]), (mown_hbm.at[r, :], mown_ref.at[r, :]), (cot_hbm.at[r, :], cot_ref.at[r, :])]
        blocks.append(launch(pairs, in_sem, 3 + 3 * b))
    first = at_hbm.shape[0] - hub_ref.shape[0]
    hub_load = pltpu.make_async_copy(at_hbm.at[first:, :], hub_ref, in_sem.at[3 + 3 * steps])

    @pl.when(core_ref[0] != 0)
    def _():
        hub_load.start()

    for copy in early:
        copy.wait()
    pre_ref[...] = mm(f_ref[...], w_ref[:width, :])
    for copy in loads:
        copy.wait()
    w2 = w_ref[width:, :]
    stores = []
    for b, r in enumerate(rows):
        for copy in blocks[b]:
            copy.wait()
        mean = ((mm_first(mix_ref[b], recv_ref[...]) + mown_ref[r, :]) / DEG).astype(BF)
        mean_ref[r, :] = mean
        pre = pre_ref[r, :] + mm(mean, w2)
        sig = jax.nn.sigmoid(pre)
        act_ref[r, :] = (pre * sig).astype(BF)
        delta = (cot_ref[r, :].astype(F32) * sig * (1.0 + pre * (1.0 - sig))).astype(BF)
        delta_ref[r, :] = delta
        gm_ref[r, :] = (mm_last(delta, w2) / DEG).astype(BF)
        stores += launch(
            [(x.at[r, :], y.at[r, :]) for x, y in
             ((gm_ref, gm_hbm), (act_ref, act_hbm), (delta_ref, delta_hbm), (mean_ref, mean_hbm))],
            out_sem, 4 * b,
        )
    half = width
    tops = [slice(0, half), slice(half, 2 * half)]

    @pl.when(core_ref[0] == 0)
    def _():
        for i, (r, x) in enumerate(zip(tops, (f_ref, mean_ref))):
            give_ref[r, :] = mm_first(x[...], delta_ref[...]).astype(BF)
            pltpu.make_async_copy(give_ref.at[r, :], give_hbm.at[r, :], out_sem.at[4 * steps + i]).start()

    @pl.when(core_ref[0] != 0)
    def _():
        hub_load.wait()
        for i, r in enumerate(tops):
            give_ref[r, :] = mm(hub_ref[r, :], gm_ref[...]).astype(BF)
            pltpu.make_async_copy(give_ref.at[r, :], give_hbm.at[r, :], out_sem.at[4 * steps + i]).start()

    for i, r in enumerate(tops):
        pltpu.make_async_copy(give_ref.at[r, :], give_hbm.at[r, :], out_sem.at[4 * steps + i]).wait()
    for copy in stores:
        copy.wait()


def keep_kernel(core_ref, gm_hbm, at_hbm, f_hbm, mean_hbm, delta_hbm, keep_hbm,
                gm_ref, at_ref, f_ref, mean_ref, delta_ref, keep_ref, in_sem, out_sem):
    nodes, width = f_ref.shape
    halo = at_ref.shape[0]
    tops = [slice(0, width), slice(width, 2 * width)]

    @pl.when(core_ref[0] == 0)
    def _():
        first = at_hbm.shape[0] - halo
        loads = launch([(gm_hbm, gm_ref)] + [(at_hbm.at[first + r.start : first + r.stop, :], at_ref.at[r, :]) for r in tops], in_sem)
        loads[0].wait()
        stores = []
        for i, r in enumerate(tops):
            loads[1 + i].wait()
            keep_ref[r, :] = mm(at_ref[r, :], gm_ref[...]).astype(BF)
            stores += launch([(keep_ref.at[r, :], keep_hbm.at[r, :])], out_sem, i)
        for copy in stores:
            copy.wait()

    @pl.when(core_ref[0] != 0)
    def _():
        loads = launch([(delta_hbm, delta_ref), (f_hbm, f_ref), (mean_hbm, mean_ref)], in_sem)
        loads[0].wait()
        stores = []
        for i, (r, x) in enumerate(zip(tops, (f_ref, mean_ref))):
            loads[1 + i].wait()
            keep_ref[r, :] = mm_first(x[...], delta_ref[...]).astype(BF)
            stores += launch([(keep_ref.at[r, :], keep_hbm.at[r, :])], out_sem, i)
        for copy in stores:
            copy.wait()


def pack_kernel(gm_ref, at_ref, keep_hbm, got_ref, out_ref, keep_ref, sems):
    parts = out_ref.shape[0]
    width = out_ref.shape[2]
    step = 32
    rows = [slice(b * step * 8, (b + 1) * step * 8) for b in range(parts // step)]
    loads = launch([(keep_hbm.at[r, :], keep_ref.at[r, :]) for r in rows], sems)
    for b, r in enumerate(rows):
        listed = mm(at_ref[r, :], gm_ref[...])
        loads[b].wait()
        total = keep_ref[r, :].astype(F32) + got_ref[r, :].astype(F32)
        both = jnp.concatenate([listed.reshape(step, 8, width), total.reshape(step, 8, width)], axis=1)
        out_ref[b * step : (b + 1) * step] = both.astype(BF)


def last_kernel(st_ref, back_ref, at_ref, gm_ref, delta_ref, w_ref, hub_ref, out_hbm, weight_ref, list_ref, out_ref, sems):
    nodes, width = out_ref.shape
    step = 256
    hub_sum = jnp.zeros(weight_ref.shape, F32)
    weight_sum = jnp.zeros(weight_ref.shape, F32)
    for q in range(0, back_ref.shape[0] // 16, 2):
        even = back_ref[q * 16 : (q + 1) * 16, :].astype(F32)
        odd = back_ref[(q + 1) * 16 : (q + 2) * 16, :].astype(F32)
        hub_sum = hub_sum + even[8:, :]
        weight_sum = weight_sum + odd[8:, :]
        list_ref[q * 8 : (q + 2) * 8, :] = jnp.concatenate([even[:8, :], odd[:8, :]], axis=0).astype(BF)
    weight_ref[...] = weight_sum
    high = hub_sum.astype(BF)
    low = (hub_sum - high.astype(F32)).astype(BF)
    hub_rows = jnp.concatenate([high, low], axis=0)
    hubs = jnp.concatenate([hub_ref[...], hub_ref[...]], axis=1)
    stores = []
    for b in range(nodes // step):
        r = slice(b * step, (b + 1) * step)
        own = mm(at_ref[r, :], gm_ref[...]) + mm_last(delta_ref[r, :], w_ref[:width, :])
        hot = (iota((step, hubs.shape[1]), 0) + b * step == hubs).astype(F32).astype(BF)
        out_ref[r, :] = (own + mm(hot, hub_rows) + mm(st_ref[r, :], list_ref[...])).astype(BF)
        stores += launch([(out_ref.at[r, :], out_hbm.at[r, :])], sems, b)
    for copy in stores:
        copy.wait()


def call(kernel, ins, outs, scratch=(), flops=0, read=0, mib=60, in_specs=None, out_specs=None):
    return pl.pallas_call(
        kernel,
        out_shape=[jax.ShapeDtypeStruct(s, d) for s, d in outs],
        in_specs=in_specs or [HB] * len(ins),
        out_specs=out_specs or [HB] * len(outs),
        scratch_shapes=[pltpu.VMEM(*x) if isinstance(x, tuple) else x for x in scratch],
        compiler_params=pltpu.CompilerParams(vmem_limit_bytes=mib * MIB),
        cost_estimate=pl.CostEstimate(flops=flops, bytes_accessed=read, transcendentals=0),
    )(*ins)


def local(features, weights, cotangent, neighbours, send_rows, send_count, hub_local):
    nodes, width = features.shape
    parts = lax.axis_size(AXES)
    halo = parts * 8
    core = (lax.axis_index("col") % 2).astype(jnp.int32).reshape(1)
    sems = lambda n: pltpu.SemaphoreType.DMA((n,))
    wide, half = ((nodes, width), F32), ((nodes, width), BF)
    packed = ((parts, 16, width), BF)

    (pay,) = call(
        send_kernel,
        [features, send_rows[0].T, send_count, hub_local],
        [packed],
        [half, ((8, parts), jnp.int32), ((1, parts), jnp.int32), ((1, 8), jnp.int32), ((parts, 8), F32), packed, sems(4), sems(parts // 32)],
        flops=2 * nodes * halo * width, read=3 * MIB,
    )
    recv = lax.all_to_all(pay, AXES, split_axis=0, concat_axis=0, tiled=True).reshape(2 * halo, width)

    live = iota((parts, 8), 1) < send_count[0][:, None]
    slot = jnp.where(live, send_rows[0], -1).reshape(1, halo)
    square = ((nodes, nodes), BF)
    hot = [square, ((halo, nodes), BF), ((halo, nodes), BF), ((2, 2 * halo, nodes // 2), BF), ((nodes, halo), BF), wide]
    at_own, at_halo, at, mix, st, mean_own = call(
        hot_kernel, [neighbours.T, slot, features], hot, hot + [sems(6)],
        flops=14 * 10**9, read=20 * MIB, mib=63, in_specs=[VM] * 3,
    )
    both = ((2 * width, width), BF)
    mid = [half, half, half, half, both]
    act, delta, gm, mean, give = call(
        mid_kernel,
        [core, recv, mix, at, mean_own, weights, features, cotangent],
        mid,
        [((2 * halo, width), BF), ((2, 2 * halo, nodes // 2), BF), ((halo, nodes), BF), wide, both, half, half, wide]
        + mid + [sems(16), sems(18)],
        flops=6 * 10**9, read=16 * MIB, in_specs=[SM] + [HB] * 7,
    )
    got = lax.ppermute(give, AXES, [(i, i ^ 1) for i in range(parts)])
    (keep,) = call(
        keep_kernel, [core, gm, at, features, mean, delta], [((24 * halo, width), BF)],
        [half, ((halo, nodes), BF), half, half, half, ((halo, width), BF), sems(3), sems(2)],
        flops=2 * 10**9, read=8 * MIB, mib=56, in_specs=[SM] + [HB] * 5,
    )
    (pay_back,) = call(
        pack_kernel, [gm, at_halo, keep, got], [packed], [((halo, width), BF), sems(parts // 32)],
        flops=10**9, read=6 * MIB, mib=44, in_specs=[VM, VM, HB, VM], out_specs=[VM],
    )
    back = lax.all_to_all(pay_back, AXES, split_axis=0, concat_axis=0, tiled=True).reshape(2 * halo, width)
    grad, grad_weights = call(
        last_kernel, [st, back, at_own, gm, delta, weights, hub_local], [half, ((8, width), F32)],
        [((halo, width), BF), half, sems(4)],
        flops=4 * 10**9, read=10 * MIB, mib=24, in_specs=[VM] * 7, out_specs=[HB, VM],
    )
    return act, grad, grad_weights


def solution(mesh):
    both = P(AXES, None)
    placed = (both, P(), both, both, P(AXES, None, None), both, both)
    return jax.shard_map(local, mesh=mesh, in_specs=placed, out_specs=(both, both, both), check_vma=False)
```

```python
import jax
import jax.numpy as jnp
from jax import lax
from jax.experimental import pallas as pl
from jax.experimental.pallas import tpu as pltpu
from jax.sharding import PartitionSpec as P

BF = jnp.bfloat16
F32 = jnp.float32
DEG = 8
BIG = 12
AXES = ("row", "col")
VM = pl.BlockSpec(memory_space=pltpu.VMEM)
SM = pl.BlockSpec(memory_space=pltpu.SMEM)
HB = pl.BlockSpec(memory_space=pltpu.HBM)
MIB = 1024 * 1024


def iota(shape, dim):
    return lax.broadcasted_iota(jnp.int32, shape, dim)


def mm(a, b):
    return jnp.dot(a, b, preferred_element_type=F32)


def mm_last(a, b):
    return lax.dot_general(a, b, (((1,), (1,)), ((), ())), preferred_element_type=F32)


def mm_first(a, b):
    return lax.dot_general(a, b, (((0,), (0,)), ((), ())), preferred_element_type=F32)


def send_kernel(f_hbm, rows_hbm, count_hbm, hub_hbm, out_hbm, f_ref, rows_ref, count_ref, hub_ref, idx_ref, out_ref, sem, out_sem):
    loads = [
        pltpu.make_async_copy(src, dst, sem.at[i])
        for i, (src, dst) in enumerate(
            ((f_hbm, f_ref), (rows_hbm, rows_ref), (count_hbm, count_ref), (hub_hbm, hub_ref))
        )
    ]
    for copy in loads:
        copy.start()
    for copy in loads[1:]:
        copy.wait()
    parts = rows_ref.shape[1]
    nodes = f_ref.shape[0]
    live = iota((8, parts), 0) < count_ref[...]
    idx = jnp.where(live, rows_ref[...], -1).astype(F32)
    idx_ref[...] = idx.T
    hub = jnp.broadcast_to(hub_ref[...], (8, 8))
    hub_col = jnp.sum(jnp.where(iota((8, 8), 0) == iota((8, 8), 1), hub, 0), axis=1, keepdims=True)
    hub_hot = (iota((8, nodes), 1) == hub_col).astype(F32).astype(BF)
    loads[0].wait()
    hub_rows = mm(hub_hot, f_ref[...])
    step = 32
    stores = []
    for b in range(parts // step):
        blk = idx_ref[b * step : (b + 1) * step, :]
        wide = jnp.broadcast_to(blk[:, None, :], (step, 8, 8)).reshape(step * 8, 8)
        pick = iota((step * 8, 8), 0) % 8 == iota((step * 8, 8), 1)
        col = jnp.sum(jnp.where(pick, wide, 0.0), axis=1, keepdims=True).astype(jnp.int32)
        hot = (iota((step * 8, nodes), 1) == col).astype(F32).astype(BF)
        listed = mm(hot, f_ref[...]).reshape(step, 8, -1)
        both = jnp.concatenate(
            [listed, jnp.broadcast_to(hub_rows[None], (step, 8, hub_rows.shape[1]))], axis=1
        )
        at = slice(b * step, (b + 1) * step)
        out_ref[at] = both.astype(BF)
        stores.append(pltpu.make_async_copy(out_ref.at[at], out_hbm.at[at], out_sem.at[b]))
        stores[-1].start()
    for copy in stores:
        copy.wait()


def unique(t):
    keep, count = [], []
    for k in range(DEG):
        row = t[k : k + 1]
        total = jnp.zeros_like(row)
        seen = None
        for j in range(DEG):
            same = t[j : j + 1] == row
            total = total + jnp.where(same, 1.0, 0.0)
            if j < k:
                seen = same if seen is None else seen | same
        keep.append(row if seen is None else jnp.where(seen, -1.0, row))
        count.append(total)
    return jnp.concatenate(keep, axis=0), jnp.concatenate(count, axis=0)


def count_matrix(u, m, outs):
    span = 256
    first = 0
    for out_ref in outs:
        lanes = out_ref.shape[1]
        at = slice(first, first + lanes)
        first += lanes
        counts = [jnp.broadcast_to(m[k : k + 1, at], (16, lanes)).astype(BF) for k in range(DEG)]
        base = iota((16, lanes), 0).astype(F32).astype(BF)

        @pl.loop(0, out_ref.shape[0] // span)
        def _(b):
            near = jnp.clip(u[:, at] - (b * span).astype(F32), -1.0, float(span))
            names = [jnp.broadcast_to(near[k : k + 1], (16, lanes)).astype(BF) for k in range(DEG)]
            for h in range(0, span, 16):
                it = base + BF(h)
                acc = jnp.zeros((16, lanes), BF)
                for k in range(DEG):
                    acc = jnp.where(it == names[k], counts[k], acc)
                out_ref[pl.ds(pl.multiple_of(b * span + h, 16), 16), :] = acc


def launch(pairs, sems, first=0):
    copies = [pltpu.make_async_copy(src, dst, sems.at[first + i]) for i, (src, dst) in enumerate(pairs)]
    for copy in copies:
        copy.start()
    return copies


def hot_kernel(nb_ref, slot_ref, f_ref, own_hbm, listed_hbm, hub_hbm, mix_hbm, st_hbm, mown_hbm,
               own_ref, listed_ref, hub_ref, mix_ref, st_ref, mown_ref, sems):
    nodes = f_ref.shape[0]
    halo = hub_ref.shape[0]
    half = nodes // 2
    cols = [slice(0, half), slice(half, nodes)]
    u, m = unique(nb_ref[...].astype(F32))
    w = u.astype(jnp.int32) - nodes
    is_hub = w >= halo
    v = jnp.where(is_hub, w - halo, w)
    v = (v // 8) * 16 + v % 8 + jnp.where(is_hub, 8, 0)
    count_matrix(jnp.where(w < 0, -1, v).astype(F32), m, [mix_ref.at[c] for c in range(mix_ref.shape[0])])
    copies = launch([(mix_ref, mix_hbm)], sems, 0)
    count_matrix(u, m, [own_ref.at[:, c] for c in cols])
    mown_ref[...] = mm_first(own_ref[...], f_ref[...])
    copies += launch([(own_ref, own_hbm), (mown_ref, mown_hbm)], sems, 1)
    count_matrix(u - nodes, m, [listed_ref.at[:, c] for c in cols])
    count_matrix(u - (nodes + halo), m, [hub_ref.at[:, c] for c in cols])
    copies += launch([(listed_ref, listed_hbm), (hub_ref, hub_hbm.at[:halo, :])], sems, 3)
    slot = slot_ref[...]

    @pl.loop(0, nodes // 16)
    def _(b):
        it = iota((16, slot.shape[1]), 0) + b * 16
        st_ref[pl.ds(pl.multiple_of(b * 16, 16), 16), :] = (it == slot).astype(F32).astype(BF)

    copies += launch([(st_ref, st_hbm)], sems, 5)
    for copy in copies:
        copy.wait()


def mid_kernel(core_ref, recv_hbm, mix_hbm, at_hbm, mown_hbm, w_hbm, f_hbm, cot_hbm,
               act_hbm, delta_hbm, gm_hbm, trio_hbm, give_hbm,
               recv_ref, mix_ref, hub_ref, mown_ref, w_ref, f_ref, cot_ref, pre_ref,
               act_ref, delta_ref, gm_ref, mean_ref, give_ref, in_sem, out_sem):
    nodes, width = delta_ref.shape
    step = 512
    steps = nodes // step
    rows = [slice(b * step, (b + 1) * step) for b in range(steps)]
    early = launch([(w_hbm, w_ref), (f_hbm, f_ref)], in_sem, 0)
    loads = launch([(recv_hbm, recv_ref)], in_sem, 2)
    blocks = []
    for b, r in enumerate(rows):
        pairs = [(mix_hbm.at[b], mix_ref.at[b]), (mown_hbm.at[r, :], mown_ref.at[r, :]), (cot_hbm.at[r, :], cot_ref.at[r, :])]
        blocks.append(launch(pairs, in_sem, 3 + 3 * b))
    hub_load = pltpu.make_async_copy(at_hbm.at[: hub_ref.shape[0], :], hub_ref, in_sem.at[3 + 3 * steps])

    @pl.when(core_ref[0] != 0)
    def _():
        hub_load.start()

    for copy in early:
        copy.wait()
    pre_ref[...] = mm(f_ref[...], w_ref[:width, :])
    for copy in loads:
        copy.wait()
    w2 = w_ref[width:, :]
    stores = []
    for b, r in enumerate(rows):
        for copy in blocks[b]:
            copy.wait()
        mean = ((mm_first(mix_ref[b], recv_ref[...]) + mown_ref[r, :]) / DEG).astype(BF)
        mean_ref[r, :] = mean
        pre = pre_ref[r, :] + mm(mean, w2)
        sig = jax.nn.sigmoid(pre)
        act_ref[r, :] = (pre * sig).astype(BF)
        delta = (cot_ref[r, :].astype(F32) * sig * (1.0 + pre * (1.0 - sig))).astype(BF)
        delta_ref[r, :] = delta
        gm_ref[r, :] = (mm_last(delta, w2) / DEG).astype(BF)
        stores += launch(
            [(x.at[r, :], y.at[r, :]) for x, y in ((gm_ref, gm_hbm), (act_ref, act_hbm), (delta_ref, delta_hbm))]
            + [
                (x.at[r, :], trio_hbm.at[i * nodes + r.start : i * nodes + r.stop, :])
                for i, x in enumerate((gm_ref, delta_ref, mean_ref))
            ],
            out_sem, 6 * b,
        )

    half = width
    tops = [slice(0, half), slice(half, 2 * half)]

    @pl.when(core_ref[0] == 0)
    def _():
        for i, (r, x) in enumerate(zip(tops, (f_ref, mean_ref))):
            give_ref[r, :] = mm_first(x[...], delta_ref[...]).astype(BF)
            pltpu.make_async_copy(give_ref.at[r, :], give_hbm.at[r, :], out_sem.at[6 * steps + i]).start()

    @pl.when(core_ref[0] != 0)
    def _():
        hub_load.wait()
        for i, r in enumerate(tops):
            give_ref[r, :] = mm(hub_ref[r, :], gm_ref[...]).astype(BF)
            pltpu.make_async_copy(give_ref.at[r, :], give_hbm.at[r, :], out_sem.at[6 * steps + i]).start()

    for i, r in enumerate(tops):
        pltpu.make_async_copy(give_ref.at[r, :], give_hbm.at[r, :], out_sem.at[6 * steps + i]).wait()
    for copy in stores:
        copy.wait()


def pack_kernel(core_ref, trio_hbm, at_ref, hub_hbm, f_ref, got_ref, out_ref, gm_ref, delta_ref, mean_ref, hub_ref, sems):
    parts, _, width = out_ref.shape
    nodes = gm_ref.shape[0]
    step = 32
    rows = [slice(b * step * 8, (b + 1) * step * 8) for b in range(parts // step)]

    def fill(sources, own):
        loads = launch(sources, sems)
        loads[0].wait()
        listed = mm(at_ref[...], gm_ref[...])
        for load in loads[1:]:
            load.wait()
        for b, r in enumerate(rows):
            total = own(r) + got_ref[r, :].astype(F32)
            both = jnp.concatenate([listed[r, :].reshape(step, 8, width), total.reshape(step, 8, width)], axis=1)
            out_ref[b * step : (b + 1) * step] = both.astype(BF)

    gm_load = (trio_hbm.at[:nodes, :], gm_ref)

    def weight_rows(r):
        x_ref = f_ref if r.start < width else mean_ref
        first = r.start % width
        return mm_first(x_ref[:, first : first + step * 8], delta_ref[...])

    @pl.when(core_ref[0] == 0)
    def _():
        fill([gm_load, (hub_hbm.at[: hub_ref.shape[0], :], hub_ref)], lambda r: mm(hub_ref[r, :], gm_ref[...]))

    @pl.when(core_ref[0] != 0)
    def _():
        fill(
            [gm_load] + [(trio_hbm.at[i * nodes : (i + 1) * nodes, :], x) for i, x in ((1, delta_ref), (2, mean_ref))],
            weight_rows,
        )


def last_kernel(st_ref, back_ref, at_ref, gm_ref, delta_ref, w_ref, hub_ref, out_hbm, weight_ref, list_ref, out_ref, sems):
    nodes, width = out_ref.shape
    step = 256
    hub_sum = jnp.zeros(weight_ref.shape, F32)
    weight_sum = jnp.zeros(weight_ref.shape, F32)
    for q in range(0, back_ref.shape[0] // 16, 2):
        even = back_ref[q * 16 : (q + 1) * 16, :].astype(F32)
        odd = back_ref[(q + 1) * 16 : (q + 2) * 16, :].astype(F32)
        hub_sum = hub_sum + even[8:, :]
        weight_sum = weight_sum + odd[8:, :]
        list_ref[q * 8 : (q + 2) * 8, :] = jnp.concatenate([even[:8, :], odd[:8, :]], axis=0).astype(BF)
    weight_ref[...] = weight_sum
    high = hub_sum.astype(BF)
    low = (hub_sum - high.astype(F32)).astype(BF)
    hub_rows = jnp.concatenate([high, low], axis=0)
    hubs = jnp.concatenate([hub_ref[...], hub_ref[...]], axis=1)
    stores = []
    for b in range(nodes // step):
        r = slice(b * step, (b + 1) * step)
        own = mm(at_ref[r, :], gm_ref[...]) + mm_last(delta_ref[r, :], w_ref[:width, :])
        hot = (iota((step, hubs.shape[1]), 0) + b * step == hubs).astype(F32).astype(BF)
        out_ref[r, :] = (own + mm(hot, hub_rows) + mm(st_ref[r, :], list_ref[...])).astype(BF)
        stores += launch([(out_ref.at[r, :], out_hbm.at[r, :])], sems, b)
    for copy in stores:
        copy.wait()


def call(kernel, ins, outs, scratch=(), flops=0, read=0, mib=60, in_specs=None, out_specs=None):
    return pl.pallas_call(
        kernel,
        out_shape=[jax.ShapeDtypeStruct(s, d) for s, d in outs],
        in_specs=in_specs or [HB] * len(ins),
        out_specs=out_specs or [HB] * len(outs),
        scratch_shapes=[pltpu.VMEM(*x) if isinstance(x, tuple) else x for x in scratch],
        compiler_params=pltpu.CompilerParams(vmem_limit_bytes=mib * MIB),
        cost_estimate=pl.CostEstimate(flops=flops, bytes_accessed=read, transcendentals=0),
    )(*ins)


def local(features, weights, cotangent, neighbours, send_rows, send_count, hub_local):
    nodes, width = features.shape
    parts = lax.axis_size(AXES)
    halo = parts * 8
    core = (lax.axis_index("col") % 2).astype(jnp.int32).reshape(1)
    sems = lambda n: pltpu.SemaphoreType.DMA((n,))
    wide, half = ((nodes, width), F32), ((nodes, width), BF)
    packed = ((parts, 16, width), BF)

    (pay,) = call(
        send_kernel,
        [features, send_rows[0].T, send_count, hub_local],
        [packed],
        [half, ((8, parts), jnp.int32), ((1, parts), jnp.int32), ((1, 8), jnp.int32), ((parts, 8), F32), packed, sems(4), sems(parts // 32)],
        flops=2 * nodes * halo * width, read=3 * MIB,
    )
    recv = lax.all_to_all(pay, AXES, split_axis=0, concat_axis=0, tiled=True).reshape(2 * halo, width)

    live = iota((parts, 8), 1) < send_count[0][:, None]
    slot = jnp.where(live, send_rows[0], -1).reshape(1, halo)
    square = ((nodes, nodes), BF)
    hot = [square, ((halo, nodes), BF), ((halo, nodes), BF), ((2, 2 * halo, nodes // 2), BF), ((nodes, halo), BF), wide]
    outs = hot[:2] + [((BIG * halo, nodes), BF)] + hot[3:]
    at_own, at_halo, at, mix, st, mean_own = call(
        hot_kernel, [neighbours.T, slot, features], outs, hot + [sems(6)],
        flops=14 * 10**9, read=20 * MIB, mib=63, in_specs=[VM] * 3,
    )
    both = ((2 * width, width), BF)
    mid = [half, half, half, half, both]
    act, delta, gm, trio, give = call(
        mid_kernel,
        [core, recv, mix, at, mean_own, weights, features, cotangent],
        mid[:3] + [((2 * BIG * nodes, width), BF), both],
        [((2 * halo, width), BF), ((2, 2 * halo, nodes // 2), BF), ((halo, nodes), BF), wide, both, half, half, wide]
        + mid + [sems(16), sems(18)],
        flops=6 * 10**9, read=16 * MIB, in_specs=[SM] + [HB] * 7,
    )
    got = lax.ppermute(give, AXES, [(i, i ^ 1) for i in range(parts)])
    (pay_back,) = call(
        pack_kernel, [core, trio, at_halo, at, features, got], [packed],
        [half, half, half, ((halo, nodes), BF), sems(3)],
        flops=2 * 10**9, read=6 * MIB, mib=40, in_specs=[SM, HB, VM, HB, VM, VM], out_specs=[VM],
    )
    back = lax.all_to_all(pay_back, AXES, split_axis=0, concat_axis=0, tiled=True).reshape(2 * halo, width)
    grad, grad_weights = call(
        last_kernel, [st, back, at_own, gm, delta, weights, hub_local], [half, ((8, width), F32)],
        [((halo, width), BF), half, sems(4)],
        flops=4 * 10**9, read=10 * MIB, mib=24, in_specs=[VM] * 7, out_specs=[HB, VM],
    )
    return act, grad, grad_weights


def solution(mesh):
    both = P(AXES, None)
    placed = (both, P(), both, both, P(AXES, None, None), both, both)
    return jax.shard_map(local, mesh=mesh, in_specs=placed, out_specs=(both, both, both), check_vma=False)
```

```python
import jax
import jax.numpy as jnp
from jax import lax
from jax.experimental import pallas as pl
from jax.experimental.pallas import tpu as pltpu
from jax.sharding import PartitionSpec as P

BF = jnp.bfloat16
F32 = jnp.float32
DEG = 8
BIG = 12
AXES = ("row", "col")
VM = pl.BlockSpec(memory_space=pltpu.VMEM)
SM = pl.BlockSpec(memory_space=pltpu.SMEM)
HB = pl.BlockSpec(memory_space=pltpu.HBM)
MIB = 1024 * 1024


def iota(shape, dim):
    return lax.broadcasted_iota(jnp.int32, shape, dim)


def mm(a, b):
    return jnp.dot(a, b, preferred_element_type=F32)


def mm_last(a, b):
    return lax.dot_general(a, b, (((1,), (1,)), ((), ())), preferred_element_type=F32)


def mm_first(a, b):
    return lax.dot_general(a, b, (((0,), (0,)), ((), ())), preferred_element_type=F32)


def send_kernel(f_hbm, rows_hbm, count_hbm, hub_hbm, out_hbm, f_ref, rows_ref, count_ref, hub_ref, idx_ref, out_ref, sem, out_sem):
    loads = [
        pltpu.make_async_copy(src, dst, sem.at[i])
        for i, (src, dst) in enumerate(
            ((f_hbm, f_ref), (rows_hbm, rows_ref), (count_hbm, count_ref), (hub_hbm, hub_ref))
        )
    ]
    for copy in loads:
        copy.start()
    for copy in loads[1:]:
        copy.wait()
    parts = rows_ref.shape[1]
    nodes = f_ref.shape[0]
    live = iota((8, parts), 0) < count_ref[...]
    idx = jnp.where(live, rows_ref[...], -1).astype(F32)
    idx_ref[...] = idx.T
    hub = jnp.broadcast_to(hub_ref[...], (8, 8))
    hub_col = jnp.sum(jnp.where(iota((8, 8), 0) == iota((8, 8), 1), hub, 0), axis=1, keepdims=True)
    hub_hot = (iota((8, nodes), 1) == hub_col).astype(F32).astype(BF)
    loads[0].wait()
    hub_rows = mm(hub_hot, f_ref[...])
    step = 32
    stores = []
    for b in range(parts // step):
        blk = idx_ref[b * step : (b + 1) * step, :]
        wide = jnp.broadcast_to(blk[:, None, :], (step, 8, 8)).reshape(step * 8, 8)
        pick = iota((step * 8, 8), 0) % 8 == iota((step * 8, 8), 1)
        col = jnp.sum(jnp.where(pick, wide, 0.0), axis=1, keepdims=True).astype(jnp.int32)
        hot = (iota((step * 8, nodes), 1) == col).astype(F32).astype(BF)
        listed = mm(hot, f_ref[...]).reshape(step, 8, -1)
        both = jnp.concatenate(
            [listed, jnp.broadcast_to(hub_rows[None], (step, 8, hub_rows.shape[1]))], axis=1
        )
        at = slice(b * step, (b + 1) * step)
        out_ref[at] = both.astype(BF)
        stores.append(pltpu.make_async_copy(out_ref.at[at], out_hbm.at[at], out_sem.at[b]))
        stores[-1].start()
    for copy in stores:
        copy.wait()


def unique(t):
    keep, count = [], []
    for k in range(DEG):
        row = t[k : k + 1]
        total = jnp.zeros_like(row)
        seen = None
        for j in range(DEG):
            same = t[j : j + 1] == row
            total = total + jnp.where(same, 1.0, 0.0)
            if j < k:
                seen = same if seen is None else seen | same
        keep.append(row if seen is None else jnp.where(seen, -1.0, row))
        count.append(total)
    return jnp.concatenate(keep, axis=0), jnp.concatenate(count, axis=0)


def count_matrix(u, m, outs):
    span = 256
    first = 0
    for out_ref in outs:
        lanes = out_ref.shape[1]
        at = slice(first, first + lanes)
        first += lanes
        counts = [jnp.broadcast_to(m[k : k + 1, at], (16, lanes)).astype(BF) for k in range(DEG)]
        base = iota((16, lanes), 0).astype(F32).astype(BF)

        @pl.loop(0, out_ref.shape[0] // span)
        def _(b):
            near = jnp.clip(u[:, at] - (b * span).astype(F32), -1.0, float(span))
            names = [jnp.broadcast_to(near[k : k + 1], (16, lanes)).astype(BF) for k in range(DEG)]
            for h in range(0, span, 16):
                it = base + BF(h)
                acc = jnp.zeros((16, lanes), BF)
                for k in range(DEG):
                    acc = jnp.where(it == names[k], counts[k], acc)
                out_ref[pl.ds(pl.multiple_of(b * span + h, 16), 16), :] = acc


def launch(pairs, sems, first=0):
    copies = [pltpu.make_async_copy(src, dst, sems.at[first + i]) for i, (src, dst) in enumerate(pairs)]
    for copy in copies:
        copy.start()
    return copies


def hot_kernel(nb_ref, slot_ref, f_ref, own_hbm, listed_hbm, hub_hbm, mix_hbm, st_hbm, mown_hbm,
               own_ref, listed_ref, hub_ref, mix_ref, st_ref, mown_ref, sems):
    nodes = f_ref.shape[0]
    halo = hub_ref.shape[0]
    half = nodes // 2
    cols = [slice(0, half), slice(half, nodes)]
    u, m = unique(nb_ref[...].astype(F32))
    w = u.astype(jnp.int32) - nodes
    is_hub = w >= halo
    v = jnp.where(is_hub, w - halo, w)
    v = (v // 8) * 16 + v % 8 + jnp.where(is_hub, 8, 0)
    count_matrix(jnp.where(w < 0, -1, v).astype(F32), m, [mix_ref.at[c] for c in range(mix_ref.shape[0])])
    copies = launch([(mix_ref, mix_hbm)], sems, 0)
    count_matrix(u, m, [own_ref.at[:, c] for c in cols])
    mown_ref[...] = mm_first(own_ref[...], f_ref[...])
    copies += launch([(own_ref, own_hbm), (mown_ref, mown_hbm)], sems, 1)
    count_matrix(u - nodes, m, [listed_ref.at[:, c] for c in cols])
    count_matrix(u - (nodes + halo), m, [hub_ref.at[:, c] for c in cols])
    copies += launch([(listed_ref, listed_hbm), (hub_ref, hub_hbm.at[:halo, :])], sems, 3)
    slot = slot_ref[...]

    @pl.loop(0, nodes // 16)
    def _(b):
        it = iota((16, slot.shape[1]), 0) + b * 16
        st_ref[pl.ds(pl.multiple_of(b * 16, 16), 16), :] = (it == slot).astype(F32).astype(BF)

    copies += launch([(st_ref, st_hbm)], sems, 5)
    for copy in copies:
        copy.wait()


def mid_kernel(core_ref, recv_hbm, mix_hbm, at_hbm, mown_hbm, w_hbm, f_hbm, cot_hbm,
               act_hbm, delta_hbm, gm_hbm, trio_hbm, give_hbm,
               recv_ref, mix_ref, hub_ref, mown_ref, w_ref, f_ref, cot_ref, pre_ref,
               act_ref, delta_ref, gm_ref, mean_ref, give_ref, in_sem, out_sem):
    nodes, width = delta_ref.shape
    step = 512
    steps = nodes // step
    rows = [slice(b * step, (b + 1) * step) for b in range(steps)]
    early = launch([(w_hbm, w_ref), (f_hbm, f_ref)], in_sem, 0)
    loads = launch([(recv_hbm, recv_ref)], in_sem, 2)
    blocks = []
    for b, r in enumerate(rows):
        pairs = [(mix_hbm.at[b], mix_ref.at[b]), (mown_hbm.at[r, :], mown_ref.at[r, :]), (cot_hbm.at[r, :], cot_ref.at[r, :])]
        blocks.append(launch(pairs, in_sem, 3 + 3 * b))
    hub_load = pltpu.make_async_copy(at_hbm.at[: hub_ref.shape[0], :], hub_ref, in_sem.at[3 + 3 * steps])

    @pl.when(core_ref[0] != 0)
    def _():
        hub_load.start()

    for copy in early:
        copy.wait()
    pre_ref[...] = mm(f_ref[...], w_ref[:width, :])
    for copy in loads:
        copy.wait()
    w2 = w_ref[width:, :]
    stores = []
    for b, r in enumerate(rows):
        for copy in blocks[b]:
            copy.wait()
        mean = ((mm_first(mix_ref[b], recv_ref[...]) + mown_ref[r, :]) / DEG).astype(BF)
        mean_ref[r, :] = mean
        pre = pre_ref[r, :] + mm(mean, w2)
        sig = jax.nn.sigmoid(pre)
        act_ref[r, :] = (pre * sig).astype(BF)
        delta = (cot_ref[r, :].astype(F32) * sig * (1.0 + pre * (1.0 - sig))).astype(BF)
        delta_ref[r, :] = delta
        gm_ref[r, :] = (mm_last(delta, w2) / DEG).astype(BF)
        stores += launch(
            [(x.at[r, :], y.at[r, :]) for x, y in ((gm_ref, gm_hbm), (act_ref, act_hbm), (delta_ref, delta_hbm))]
            + [
                (x.at[r, :], trio_hbm.at[i * nodes + r.start : i * nodes + r.stop, :])
                for i, x in enumerate((gm_ref, delta_ref, mean_ref))
            ],
            out_sem, 6 * b,
        )

    half = width
    tops = [slice(0, half), slice(half, 2 * half)]

    @pl.when(core_ref[0] == 0)
    def _():
        for i, (r, x) in enumerate(zip(tops, (f_ref, mean_ref))):
            give_ref[r, :] = mm_first(x[...], delta_ref[...]).astype(BF)
            pltpu.make_async_copy(give_ref.at[r, :], give_hbm.at[r, :], out_sem.at[6 * steps + i]).start()

    @pl.when(core_ref[0] != 0)
    def _():
        hub_load.wait()
        for i, r in enumerate(tops):
            give_ref[r, :] = mm(hub_ref[r, :], gm_ref[...]).astype(BF)
            pltpu.make_async_copy(give_ref.at[r, :], give_hbm.at[r, :], out_sem.at[6 * steps + i]).start()

    for i, r in enumerate(tops):
        pltpu.make_async_copy(give_ref.at[r, :], give_hbm.at[r, :], out_sem.at[6 * steps + i]).wait()
    for copy in stores:
        copy.wait()


def listed_kernel(trio_hbm, at_ref, out_ref, gm_ref, sem):
    (load,) = launch([(trio_hbm.at[: gm_ref.shape[0], :], gm_ref)], sem)
    load.wait()
    out_ref[...] = mm(at_ref[...], gm_ref[...]).astype(BF)


def pack_kernel(core_ref, trio_hbm, listed_ref, hub_hbm, f_ref, got_ref, out_ref, gm_ref, delta_ref, mean_ref, hub_ref, sems):
    parts, _, width = out_ref.shape
    nodes = gm_ref.shape[0]
    step = 32
    rows = [slice(b * step * 8, (b + 1) * step * 8) for b in range(parts // step)]
    parts_of = [trio_hbm.at[i * nodes : (i + 1) * nodes, :] for i in range(3)]

    def fill(own):
        for b, r in enumerate(rows):
            total = own(b, r) + got_ref[r, :].astype(F32)
            listed = listed_ref[r, :].astype(F32)
            both = jnp.concatenate([listed.reshape(step, 8, width), total.reshape(step, 8, width)], axis=1)
            out_ref[b * step : (b + 1) * step] = both.astype(BF)

    @pl.when(core_ref[0] == 0)
    def _():
        loads = launch([(parts_of[0], gm_ref)] + [(hub_hbm.at[r, :], hub_ref.at[r, :]) for r in rows], sems)
        loads[0].wait()

        def hub_rows(b, r):
            loads[1 + b].wait()
            return mm(hub_ref[r, :], gm_ref[...])

        fill(hub_rows)

    @pl.when(core_ref[0] != 0)
    def _():
        loads = launch([(parts_of[1], delta_ref), (parts_of[2], mean_ref)], sems)

        def weight_rows(b, r):
            first = r.start % width
            if b == 0:
                loads[0].wait()
            if r.start == width:
                loads[1].wait()
            x_ref = f_ref if r.start < width else mean_ref
            return mm_first(x_ref[:, first : first + step * 8], delta_ref[...])

        fill(weight_rows)


def last_kernel(st_ref, back_ref, at_ref, gm_ref, delta_ref, w_ref, hub_ref, out_hbm, weight_ref, list_ref, out_ref, sems):
    nodes, width = out_ref.shape
    step = 256
    hub_sum = jnp.zeros(weight_ref.shape, F32)
    weight_sum = jnp.zeros(weight_ref.shape, F32)
    for q in range(0, back_ref.shape[0] // 16, 2):
        even = back_ref[q * 16 : (q + 1) * 16, :].astype(F32)
        odd = back_ref[(q + 1) * 16 : (q + 2) * 16, :].astype(F32)
        hub_sum = hub_sum + even[8:, :]
        weight_sum = weight_sum + odd[8:, :]
        list_ref[q * 8 : (q + 2) * 8, :] = jnp.concatenate([even[:8, :], odd[:8, :]], axis=0).astype(BF)
    weight_ref[...] = weight_sum
    high = hub_sum.astype(BF)
    low = (hub_sum - high.astype(F32)).astype(BF)
    hub_rows = jnp.concatenate([high, low], axis=0)
    hubs = jnp.concatenate([hub_ref[...], hub_ref[...]], axis=1)
    stores = []
    for b in range(nodes // step):
        r = slice(b * step, (b + 1) * step)
        own = mm(at_ref[r, :], gm_ref[...]) + mm_last(delta_ref[r, :], w_ref[:width, :])
        hot = (iota((step, hubs.shape[1]), 0) + b * step == hubs).astype(F32).astype(BF)
        out_ref[r, :] = (own + mm(hot, hub_rows) + mm(st_ref[r, :], list_ref[...])).astype(BF)
        stores += launch([(out_ref.at[r, :], out_hbm.at[r, :])], sems, b)
    for copy in stores:
        copy.wait()


def call(kernel, ins, outs, scratch=(), flops=0, read=0, mib=60, in_specs=None, out_specs=None):
    return pl.pallas_call(
        kernel,
        out_shape=[jax.ShapeDtypeStruct(s, d) for s, d in outs],
        in_specs=in_specs or [HB] * len(ins),
        out_specs=out_specs or [HB] * len(outs),
        scratch_shapes=[pltpu.VMEM(*x) if isinstance(x, tuple) else x for x in scratch],
        compiler_params=pltpu.CompilerParams(vmem_limit_bytes=mib * MIB),
        cost_estimate=pl.CostEstimate(flops=flops, bytes_accessed=read, transcendentals=0),
    )(*ins)


def local(features, weights, cotangent, neighbours, send_rows, send_count, hub_local):
    nodes, width = features.shape
    parts = lax.axis_size(AXES)
    halo = parts * 8
    core = (lax.axis_index("col") % 2).astype(jnp.int32).reshape(1)
    sems = lambda n: pltpu.SemaphoreType.DMA((n,))
    wide, half = ((nodes, width), F32), ((nodes, width), BF)
    packed = ((parts, 16, width), BF)

    (pay,) = call(
        send_kernel,
        [features, send_rows[0].T, send_count, hub_local],
        [packed],
        [half, ((8, parts), jnp.int32), ((1, parts), jnp.int32), ((1, 8), jnp.int32), ((parts, 8), F32), packed, sems(4), sems(parts // 32)],
        flops=2 * nodes * halo * width, read=3 * MIB,
    )
    recv = lax.all_to_all(pay, AXES, split_axis=0, concat_axis=0, tiled=True).reshape(2 * halo, width)

    live = iota((parts, 8), 1) < send_count[0][:, None]
    slot = jnp.where(live, send_rows[0], -1).reshape(1, halo)
    square = ((nodes, nodes), BF)
    hot = [square, ((halo, nodes), BF), ((halo, nodes), BF), ((2, 2 * halo, nodes // 2), BF), ((nodes, halo), BF), wide]
    outs = hot[:2] + [((BIG * halo, nodes), BF)] + hot[3:]
    at_own, at_halo, at, mix, st, mean_own = call(
        hot_kernel, [neighbours.T, slot, features], outs, hot + [sems(6)],
        flops=14 * 10**9, read=20 * MIB, mib=63, in_specs=[VM] * 3,
    )
    both = ((2 * width, width), BF)
    mid = [half, half, half, half, both]
    act, delta, gm, trio, give = call(
        mid_kernel,
        [core, recv, mix, at, mean_own, weights, features, cotangent],
        mid[:3] + [((2 * BIG * nodes, width), BF), both],
        [((2 * halo, width), BF), ((2, 2 * halo, nodes // 2), BF), ((halo, nodes), BF), wide, both, half, half, wide]
        + mid + [sems(16), sems(18)],
        flops=6 * 10**9, read=16 * MIB, in_specs=[SM] + [HB] * 7,
    )
    got = lax.ppermute(give, AXES, [(i, i ^ 1) for i in range(parts)])
    (listed,) = call(
        listed_kernel, [trio, at_halo], [((halo, width), BF)], [half, sems(1)],
        flops=10**9, read=4 * MIB, mib=40, in_specs=[HB, VM], out_specs=[VM],
    )
    (pay_back,) = call(
        pack_kernel, [core, trio, listed, at, features, got], [packed],
        [half, half, half, ((halo, nodes), BF), sems(1 + parts // 32)],
        flops=2 * 10**9, read=6 * MIB, mib=40, in_specs=[SM, HB, VM, HB, VM, VM], out_specs=[VM],
    )
    back = lax.all_to_all(pay_back, AXES, split_axis=0, concat_axis=0, tiled=True).reshape(2 * halo, width)
    grad, grad_weights = call(
        last_kernel, [st, back, at_own, gm, delta, weights, hub_local], [half, ((8, width), F32)],
        [((halo, width), BF), half, sems(4)],
        flops=4 * 10**9, read=10 * MIB, mib=24, in_specs=[VM] * 7, out_specs=[HB, VM],
    )
    return act, grad, grad_weights


def solution(mesh):
    both = P(AXES, None)
    placed = (both, P(), both, both, P(AXES, None, None), both, both)
    return jax.shard_map(local, mesh=mesh, in_specs=placed, out_specs=(both, both, both), check_vma=False)
```

```python
import jax
import jax.numpy as jnp
from jax import lax
from jax.experimental import pallas as pl
from jax.experimental.pallas import tpu as pltpu
from jax.sharding import PartitionSpec as P

BF = jnp.bfloat16
F32 = jnp.float32
DEG = 8
BIG = 12
AXES = ("row", "col")
VM = pl.BlockSpec(memory_space=pltpu.VMEM)
SM = pl.BlockSpec(memory_space=pltpu.SMEM)
HB = pl.BlockSpec(memory_space=pltpu.HBM)
MIB = 1024 * 1024


def iota(shape, dim):
    return lax.broadcasted_iota(jnp.int32, shape, dim)


def mm(a, b):
    return jnp.dot(a, b, preferred_element_type=F32)


def mm_last(a, b):
    return lax.dot_general(a, b, (((1,), (1,)), ((), ())), preferred_element_type=F32)


def mm_first(a, b):
    return lax.dot_general(a, b, (((0,), (0,)), ((), ())), preferred_element_type=F32)


def send_kernel(f_hbm, rows_hbm, count_hbm, hub_hbm, out_hbm, f_ref, rows_ref, count_ref, hub_ref, idx_ref, out_ref, sem, out_sem):
    loads = [
        pltpu.make_async_copy(src, dst, sem.at[i])
        for i, (src, dst) in enumerate(
            ((f_hbm, f_ref), (rows_hbm, rows_ref), (count_hbm, count_ref), (hub_hbm, hub_ref))
        )
    ]
    for copy in loads:
        copy.start()
    for copy in loads[1:]:
        copy.wait()
    parts = rows_ref.shape[1]
    nodes = f_ref.shape[0]
    live = iota((8, parts), 0) < count_ref[...]
    idx = jnp.where(live, rows_ref[...], -1).astype(F32)
    idx_ref[...] = idx.T
    hub = jnp.broadcast_to(hub_ref[...], (8, 8))
    hub_col = jnp.sum(jnp.where(iota((8, 8), 0) == iota((8, 8), 1), hub, 0), axis=1, keepdims=True)
    hub_hot = (iota((8, nodes), 1) == hub_col).astype(F32).astype(BF)
    loads[0].wait()
    hub_rows = mm(hub_hot, f_ref[...])
    step = 32
    stores = []
    for b in range(parts // step):
        blk = idx_ref[b * step : (b + 1) * step, :]
        wide = jnp.broadcast_to(blk[:, None, :], (step, 8, 8)).reshape(step * 8, 8)
        pick = iota((step * 8, 8), 0) % 8 == iota((step * 8, 8), 1)
        col = jnp.sum(jnp.where(pick, wide, 0.0), axis=1, keepdims=True).astype(jnp.int32)
        hot = (iota((step * 8, nodes), 1) == col).astype(F32).astype(BF)
        listed = mm(hot, f_ref[...]).reshape(step, 8, -1)
        both = jnp.concatenate(
            [listed, jnp.broadcast_to(hub_rows[None], (step, 8, hub_rows.shape[1]))], axis=1
        )
        at = slice(b * step, (b + 1) * step)
        out_ref[at] = both.astype(BF)
        stores.append(pltpu.make_async_copy(out_ref.at[at], out_hbm.at[at], out_sem.at[b]))
        stores[-1].start()
    for copy in stores:
        copy.wait()


def unique(t):
    keep, count = [], []
    for k in range(DEG):
        row = t[k : k + 1]
        total = jnp.zeros_like(row)
        seen = None
        for j in range(DEG):
            same = t[j : j + 1] == row
            total = total + jnp.where(same, 1.0, 0.0)
            if j < k:
                seen = same if seen is None else seen | same
        keep.append(row if seen is None else jnp.where(seen, -1.0, row))
        count.append(total)
    return jnp.concatenate(keep, axis=0), jnp.concatenate(count, axis=0)


def count_matrix(u, m, outs):
    span = 256
    first = 0
    for out_ref in outs:
        lanes = out_ref.shape[1]
        at = slice(first, first + lanes)
        first += lanes
        counts = [jnp.broadcast_to(m[k : k + 1, at], (16, lanes)).astype(BF) for k in range(DEG)]
        base = iota((16, lanes), 0).astype(F32).astype(BF)

        @pl.loop(0, out_ref.shape[0] // span)
        def _(b):
            near = jnp.clip(u[:, at] - (b * span).astype(F32), -1.0, float(span))
            names = [jnp.broadcast_to(near[k : k + 1], (16, lanes)).astype(BF) for k in range(DEG)]
            for h in range(0, span, 16):
                it = base + BF(h)
                acc = jnp.zeros((16, lanes), BF)
                for k in range(DEG):
                    acc = jnp.where(it == names[k], counts[k], acc)
                out_ref[pl.ds(pl.multiple_of(b * span + h, 16), 16), :] = acc


def launch(pairs, sems, first=0):
    copies = [pltpu.make_async_copy(src, dst, sems.at[first + i]) for i, (src, dst) in enumerate(pairs)]
    for copy in copies:
        copy.start()
    return copies


def hot_kernel(nb_ref, slot_ref, f_ref, own_hbm, listed_hbm, hub_hbm, mix_hbm, st_hbm, mown_hbm,
               own_ref, listed_ref, hub_ref, mix_ref, st_ref, mown_ref, sems):
    nodes = f_ref.shape[0]
    halo = hub_ref.shape[0]
    half = nodes // 2
    cols = [slice(0, half), slice(half, nodes)]
    u, m = unique(nb_ref[...].astype(F32))
    w = u.astype(jnp.int32) - nodes
    is_hub = w >= halo
    v = jnp.where(is_hub, w - halo, w)
    v = (v // 8) * 16 + v % 8 + jnp.where(is_hub, 8, 0)
    count_matrix(jnp.where(w < 0, -1, v).astype(F32), m, [mix_ref.at[c] for c in range(mix_ref.shape[0])])
    copies = launch([(mix_ref, mix_hbm)], sems, 0)
    count_matrix(u, m, [own_ref.at[:, c] for c in cols])
    mown_ref[...] = mm_first(own_ref[...], f_ref[...])
    copies += launch([(own_ref, own_hbm), (mown_ref, mown_hbm)], sems, 1)
    count_matrix(u - nodes, m, [listed_ref.at[:, c] for c in cols])
    count_matrix(u - (nodes + halo), m, [hub_ref.at[:, c] for c in cols])
    copies += launch([(listed_ref, listed_hbm), (hub_ref, hub_hbm.at[:halo, :])], sems, 3)
    slot = slot_ref[...]

    @pl.loop(0, nodes // 16)
    def _(b):
        it = iota((16, slot.shape[1]), 0) + b * 16
        st_ref[pl.ds(pl.multiple_of(b * 16, 16), 16), :] = (it == slot).astype(F32).astype(BF)

    copies += launch([(st_ref, st_hbm)], sems, 5)
    for copy in copies:
        copy.wait()


def mid_kernel(core_ref, recv_hbm, mix_hbm, at_hbm, mown_hbm, w_hbm, f_hbm, cot_hbm,
               act_hbm, trio_hbm, give_hbm,
               recv_ref, mix_ref, hub_ref, mown_ref, w_ref, f_ref, cot_ref, pre_ref,
               act_ref, delta_ref, gm_ref, mean_ref, give_ref, in_sem, out_sem):
    nodes, width = delta_ref.shape
    step = 512
    steps = nodes // step
    rows = [slice(b * step, (b + 1) * step) for b in range(steps)]
    early = launch([(w_hbm, w_ref), (f_hbm, f_ref)], in_sem, 0)
    loads = launch([(recv_hbm, recv_ref)], in_sem, 2)
    blocks = []
    for b, r in enumerate(rows):
        pairs = [(mix_hbm.at[b], mix_ref.at[b]), (mown_hbm.at[r, :], mown_ref.at[r, :]), (cot_hbm.at[r, :], cot_ref.at[r, :])]
        blocks.append(launch(pairs, in_sem, 3 + 3 * b))
    hub_load = pltpu.make_async_copy(at_hbm.at[: hub_ref.shape[0], :], hub_ref, in_sem.at[3 + 3 * steps])

    @pl.when(core_ref[0] != 0)
    def _():
        hub_load.start()

    for copy in early:
        copy.wait()
    pre_ref[...] = mm(f_ref[...], w_ref[:width, :])
    for copy in loads:
        copy.wait()
    w2 = w_ref[width:, :]
    stores = []
    for b, r in enumerate(rows):
        for copy in blocks[b]:
            copy.wait()
        mean = ((mm_first(mix_ref[b], recv_ref[...]) + mown_ref[r, :]) / DEG).astype(BF)
        mean_ref[r, :] = mean
        pre = pre_ref[r, :] + mm(mean, w2)
        sig = jax.nn.sigmoid(pre)
        act_ref[r, :] = (pre * sig).astype(BF)
        delta = (cot_ref[r, :].astype(F32) * sig * (1.0 + pre * (1.0 - sig))).astype(BF)
        delta_ref[r, :] = delta
        gm_ref[r, :] = (mm_last(delta, w2) / DEG).astype(BF)
        stores += launch(
            [(act_ref.at[r, :], act_hbm.at[r, :])]
            + [
                (x.at[r, :], trio_hbm.at[i * nodes + r.start : i * nodes + r.stop, :])
                for i, x in enumerate((gm_ref, delta_ref, mean_ref))
            ],
            out_sem, 4 * b,
        )

    half = width
    tops = [slice(0, half), slice(half, 2 * half)]

    @pl.when(core_ref[0] == 0)
    def _():
        for i, (r, x) in enumerate(zip(tops, (f_ref, mean_ref))):
            give_ref[r, :] = mm_first(x[...], delta_ref[...]).astype(BF)
            pltpu.make_async_copy(give_ref.at[r, :], give_hbm.at[r, :], out_sem.at[4 * steps + i]).start()

    @pl.when(core_ref[0] != 0)
    def _():
        hub_load.wait()
        for i, r in enumerate(tops):
            give_ref[r, :] = mm(hub_ref[r, :], gm_ref[...]).astype(BF)
            pltpu.make_async_copy(give_ref.at[r, :], give_hbm.at[r, :], out_sem.at[4 * steps + i]).start()

    for i, r in enumerate(tops):
        pltpu.make_async_copy(give_ref.at[r, :], give_hbm.at[r, :], out_sem.at[4 * steps + i]).wait()
    for copy in stores:
        copy.wait()


def listed_kernel(core_ref, trio_hbm, hub_hbm, at_ref, out_ref, gm_ref, delta_ref, mean_ref, hub_ref, sems):
    nodes = gm_ref.shape[0]
    parts_of = [trio_hbm.at[i * nodes : (i + 1) * nodes, :] for i in range(3)]
    first, second = launch([(parts_of[0], gm_ref), (parts_of[1], delta_ref)], sems)
    hub_load = pltpu.make_async_copy(hub_hbm.at[: hub_ref.shape[0], :], hub_ref, sems.at[2])
    mean_load = pltpu.make_async_copy(parts_of[2], mean_ref, sems.at[3])
    even = core_ref[0] == 0
    pl.when(even)(hub_load.start)
    pl.when(jnp.logical_not(even))(mean_load.start)
    first.wait()
    out_ref[...] = mm(at_ref[...], gm_ref[...]).astype(BF)
    second.wait()
    pl.when(even)(hub_load.wait)
    pl.when(jnp.logical_not(even))(mean_load.wait)


def pack_kernel(core_ref, listed_ref, gm_ref, delta_ref, mean_ref, hub_ref, f_ref, got_ref, out_ref):
    parts, _, width = out_ref.shape
    step = 32
    rows = [slice(b * step * 8, (b + 1) * step * 8) for b in range(parts // step)]

    def fill(own):
        for b, r in enumerate(rows):
            total = own(r) + got_ref[r, :].astype(F32)
            listed = listed_ref[r, :].astype(F32)
            both = jnp.concatenate([listed.reshape(step, 8, width), total.reshape(step, 8, width)], axis=1)
            out_ref[b * step : (b + 1) * step] = both.astype(BF)

    def weight_rows(r):
        x_ref = f_ref if r.start < width else mean_ref
        first = r.start % width
        return mm_first(x_ref[:, first : first + step * 8], delta_ref[...])

    @pl.when(core_ref[0] == 0)
    def _():
        fill(lambda r: mm(hub_ref[r, :], gm_ref[...]))

    @pl.when(core_ref[0] != 0)
    def _():
        fill(weight_rows)


def last_kernel(st_ref, back_ref, at_ref, gm_ref, delta_ref, w_ref, hub_ref, out_hbm, weight_ref, list_ref, out_ref, sems):
    nodes, width = out_ref.shape
    step = 256
    hub_sum = jnp.zeros(weight_ref.shape, F32)
    weight_sum = jnp.zeros(weight_ref.shape, F32)
    for q in range(0, back_ref.shape[0] // 16, 2):
        even = back_ref[q * 16 : (q + 1) * 16, :].astype(F32)
        odd = back_ref[(q + 1) * 16 : (q + 2) * 16, :].astype(F32)
        hub_sum = hub_sum + even[8:, :]
        weight_sum = weight_sum + odd[8:, :]
        list_ref[q * 8 : (q + 2) * 8, :] = jnp.concatenate([even[:8, :], odd[:8, :]], axis=0).astype(BF)
    weight_ref[...] = weight_sum
    high = hub_sum.astype(BF)
    low = (hub_sum - high.astype(F32)).astype(BF)
    hub_rows = jnp.concatenate([high, low], axis=0)
    hubs = jnp.concatenate([hub_ref[...], hub_ref[...]], axis=1)
    stores = []
    for b in range(nodes // step):
        r = slice(b * step, (b + 1) * step)
        own = mm(at_ref[r, :], gm_ref[...]) + mm_last(delta_ref[r, :], w_ref[:width, :])
        hot = (iota((step, hubs.shape[1]), 0) + b * step == hubs).astype(F32).astype(BF)
        out_ref[r, :] = (own + mm(hot, hub_rows) + mm(st_ref[r, :], list_ref[...])).astype(BF)
        stores += launch([(out_ref.at[r, :], out_hbm.at[r, :])], sems, b)
    for copy in stores:
        copy.wait()


def call(kernel, ins, outs, scratch=(), flops=0, read=0, mib=60, in_specs=None, out_specs=None):
    return pl.pallas_call(
        kernel,
        out_shape=[jax.ShapeDtypeStruct(s, d) for s, d in outs],
        in_specs=in_specs or [HB] * len(ins),
        out_specs=out_specs or [HB] * len(outs),
        scratch_shapes=[pltpu.VMEM(*x) if isinstance(x, tuple) else x for x in scratch],
        compiler_params=pltpu.CompilerParams(vmem_limit_bytes=mib * MIB),
        cost_estimate=pl.CostEstimate(flops=flops, bytes_accessed=read, transcendentals=0),
    )(*ins)


def local(features, weights, cotangent, neighbours, send_rows, send_count, hub_local):
    nodes, width = features.shape
    parts = lax.axis_size(AXES)
    halo = parts * 8
    core = (lax.axis_index("col") % 2).astype(jnp.int32).reshape(1)
    sems = lambda n: pltpu.SemaphoreType.DMA((n,))
    wide, half = ((nodes, width), F32), ((nodes, width), BF)
    packed = ((parts, 16, width), BF)

    (pay,) = call(
        send_kernel,
        [features, send_rows[0].T, send_count, hub_local],
        [packed],
        [half, ((8, parts), jnp.int32), ((1, parts), jnp.int32), ((1, 8), jnp.int32), ((parts, 8), F32), packed, sems(4), sems(parts // 32)],
        flops=2 * nodes * halo * width, read=3 * MIB,
    )
    recv = lax.all_to_all(pay, AXES, split_axis=0, concat_axis=0, tiled=True).reshape(2 * halo, width)

    live = iota((parts, 8), 1) < send_count[0][:, None]
    slot = jnp.where(live, send_rows[0], -1).reshape(1, halo)
    square = ((nodes, nodes), BF)
    hot = [square, ((halo, nodes), BF), ((halo, nodes), BF), ((2, 2 * halo, nodes // 2), BF), ((nodes, halo), BF), wide]
    outs = hot[:2] + [((BIG * halo, nodes), BF)] + hot[3:]
    at_own, at_halo, at, mix, st, mean_own = call(
        hot_kernel, [neighbours.T, slot, features], outs, hot + [sems(6)],
        flops=14 * 10**9, read=20 * MIB, mib=63, in_specs=[VM] * 3,
    )
    both = ((2 * width, width), BF)
    mid = [half, half, half, half, both]
    act, trio, give = call(
        mid_kernel,
        [core, recv, mix, at, mean_own, weights, features, cotangent],
        [half, ((2 * BIG * nodes, width), BF), both],
        [((2 * halo, width), BF), ((2, 2 * halo, nodes // 2), BF), ((halo, nodes), BF), wide, both, half, half, wide]
        + mid + [sems(16), sems(18)],
        flops=6 * 10**9, read=16 * MIB, in_specs=[SM] + [HB] * 7,
    )
    got = lax.ppermute(give, AXES, [(i, i ^ 1) for i in range(parts)])
    listed, gm, delta, mean, hub_counts = call(
        listed_kernel, [core, trio, at, at_halo], [half, half, half, half, ((halo, nodes), BF)], [sems(4)],
        flops=10**9, read=4 * MIB, mib=24, in_specs=[SM, HB, HB, VM], out_specs=[VM] * 5,
    )
    (pay_back,) = call(
        pack_kernel, [core, listed, gm, delta, mean, hub_counts, features, got], [packed],
        flops=2 * 10**9, read=6 * MIB, mib=24, in_specs=[SM] + [VM] * 7, out_specs=[VM],
    )
    back = lax.all_to_all(pay_back, AXES, split_axis=0, concat_axis=0, tiled=True).reshape(2 * halo, width)
    grad, grad_weights = call(
        last_kernel, [st, back, at_own, gm, delta, weights, hub_local], [half, ((8, width), F32)],
        [((halo, width), BF), half, sems(4)],
        flops=4 * 10**9, read=10 * MIB, mib=24, in_specs=[VM] * 7, out_specs=[HB, VM],
    )
    return act, grad, grad_weights


def solution(mesh):
    both = P(AXES, None)
    placed = (both, P(), both, both, P(AXES, None, None), both, both)
    return jax.shard_map(local, mesh=mesh, in_specs=placed, out_specs=(both, both, both), check_vma=False)
```

```python
import jax
import jax.numpy as jnp
from jax import lax
from jax.experimental import pallas as pl
from jax.experimental.pallas import tpu as pltpu
from jax.sharding import PartitionSpec as P

BF = jnp.bfloat16
F32 = jnp.float32
DEG = 8
BIG = 12
AXES = ("row", "col")
VM = pl.BlockSpec(memory_space=pltpu.VMEM)
SM = pl.BlockSpec(memory_space=pltpu.SMEM)
HB = pl.BlockSpec(memory_space=pltpu.HBM)
MIB = 1024 * 1024


def iota(shape, dim):
    return lax.broadcasted_iota(jnp.int32, shape, dim)


def mm(a, b):
    return jnp.dot(a, b, preferred_element_type=F32)


def mm_last(a, b):
    return lax.dot_general(a, b, (((1,), (1,)), ((), ())), preferred_element_type=F32)


def mm_first(a, b):
    return lax.dot_general(a, b, (((0,), (0,)), ((), ())), preferred_element_type=F32)


def send_kernel(f_hbm, rows_hbm, count_hbm, hub_hbm, out_hbm, f_ref, rows_ref, count_ref, hub_ref, idx_ref, out_ref, sem, out_sem):
    loads = [
        pltpu.make_async_copy(src, dst, sem.at[i])
        for i, (src, dst) in enumerate(
            ((f_hbm, f_ref), (rows_hbm, rows_ref), (count_hbm, count_ref), (hub_hbm, hub_ref))
        )
    ]
    for copy in loads:
        copy.start()
    for copy in loads[1:]:
        copy.wait()
    parts = rows_ref.shape[1]
    nodes = f_ref.shape[0]
    live = iota((8, parts), 0) < count_ref[...]
    idx = jnp.where(live, rows_ref[...], -1).astype(F32)
    idx_ref[...] = idx.T
    hub = jnp.broadcast_to(hub_ref[...], (8, 8))
    hub_col = jnp.sum(jnp.where(iota((8, 8), 0) == iota((8, 8), 1), hub, 0), axis=1, keepdims=True)
    hub_hot = (iota((8, nodes), 1) == hub_col).astype(F32).astype(BF)
    loads[0].wait()
    hub_rows = mm(hub_hot, f_ref[...])
    step = 32
    stores = []
    for b in range(parts // step):
        blk = idx_ref[b * step : (b + 1) * step, :]
        wide = jnp.broadcast_to(blk[:, None, :], (step, 8, 8)).reshape(step * 8, 8)
        pick = iota((step * 8, 8), 0) % 8 == iota((step * 8, 8), 1)
        col = jnp.sum(jnp.where(pick, wide, 0.0), axis=1, keepdims=True).astype(jnp.int32)
        hot = (iota((step * 8, nodes), 1) == col).astype(F32).astype(BF)
        listed = mm(hot, f_ref[...]).reshape(step, 8, -1)
        both = jnp.concatenate(
            [listed, jnp.broadcast_to(hub_rows[None], (step, 8, hub_rows.shape[1]))], axis=1
        )
        at = slice(b * step, (b + 1) * step)
        out_ref[at] = both.astype(BF)
        stores.append(pltpu.make_async_copy(out_ref.at[at], out_hbm.at[at], out_sem.at[b]))
        stores[-1].start()
    for copy in stores:
        copy.wait()


def unique(t):
    keep, count = [], []
    for k in range(DEG):
        row = t[k : k + 1]
        total = jnp.zeros_like(row)
        seen = None
        for j in range(DEG):
            same = t[j : j + 1] == row
            total = total + jnp.where(same, 1.0, 0.0)
            if j < k:
                seen = same if seen is None else seen | same
        keep.append(row if seen is None else jnp.where(seen, -1.0, row))
        count.append(total)
    return jnp.concatenate(keep, axis=0), jnp.concatenate(count, axis=0)


def count_matrix(u, m, outs):
    span = 256
    first = 0
    for out_ref in outs:
        lanes = out_ref.shape[1]
        at = slice(first, first + lanes)
        first += lanes
        counts = [jnp.broadcast_to(m[k : k + 1, at], (16, lanes)).astype(BF) for k in range(DEG)]
        base = iota((16, lanes), 0).astype(F32).astype(BF)

        @pl.loop(0, out_ref.shape[0] // span)
        def _(b):
            near = jnp.clip(u[:, at] - (b * span).astype(F32), -1.0, float(span))
            names = [jnp.broadcast_to(near[k : k + 1], (16, lanes)).astype(BF) for k in range(DEG)]
            for h in range(0, span, 16):
                it = base + BF(h)
                acc = jnp.zeros((16, lanes), BF)
                for k in range(DEG):
                    acc = jnp.where(it == names[k], counts[k], acc)
                out_ref[pl.ds(pl.multiple_of(b * span + h, 16), 16), :] = acc


def launch(pairs, sems, first=0):
    copies = [pltpu.make_async_copy(src, dst, sems.at[first + i]) for i, (src, dst) in enumerate(pairs)]
    for copy in copies:
        copy.start()
    return copies


def hot_kernel(nb_ref, slot_ref, f_ref, own_hbm, listed_hbm, hub_hbm, mix_hbm, st_hbm, mown_hbm,
               own_ref, listed_ref, hub_ref, mix_ref, st_ref, mown_ref, sems):
    nodes = f_ref.shape[0]
    halo = hub_ref.shape[0]
    half = nodes // 2
    cols = [slice(0, half), slice(half, nodes)]
    u, m = unique(nb_ref[...].astype(F32))
    w = u.astype(jnp.int32) - nodes
    is_hub = w >= halo
    v = jnp.where(is_hub, w - halo, w)
    v = (v // 8) * 16 + v % 8 + jnp.where(is_hub, 8, 0)
    count_matrix(jnp.where(w < 0, -1, v).astype(F32), m, [mix_ref.at[c] for c in range(mix_ref.shape[0])])
    copies = launch([(mix_ref, mix_hbm)], sems, 0)
    count_matrix(u, m, [own_ref.at[:, c] for c in cols])
    mown_ref[...] = mm_first(own_ref[...], f_ref[...])
    copies += launch([(own_ref, own_hbm.at[:nodes, :]), (mown_ref, mown_hbm)], sems, 1)
    count_matrix(u - nodes, m, [listed_ref.at[:, c] for c in cols])
    count_matrix(u - (nodes + halo), m, [hub_ref.at[:, c] for c in cols])
    copies += launch([(listed_ref, listed_hbm), (hub_ref, hub_hbm.at[:halo, :])], sems, 3)
    slot = slot_ref[...]

    @pl.loop(0, nodes // 16)
    def _(b):
        it = iota((16, slot.shape[1]), 0) + b * 16
        st_ref[pl.ds(pl.multiple_of(b * 16, 16), 16), :] = (it == slot).astype(F32).astype(BF)

    copies += launch([(st_ref, st_hbm)], sems, 5)
    for copy in copies:
        copy.wait()


def mid_kernel(core_ref, recv_hbm, mix_hbm, at_hbm, mown_hbm, w_hbm, f_hbm, cot_hbm,
               act_hbm, trio_hbm, give_hbm,
               recv_ref, mix_ref, hub_ref, mown_ref, w_ref, f_ref, cot_ref, pre_ref,
               act_ref, delta_ref, gm_ref, mean_ref, give_ref, in_sem, out_sem):
    nodes, width = delta_ref.shape
    step = 512
    steps = nodes // step
    rows = [slice(b * step, (b + 1) * step) for b in range(steps)]
    early = launch([(w_hbm, w_ref), (f_hbm, f_ref)], in_sem, 0)
    loads = launch([(recv_hbm, recv_ref)], in_sem, 2)
    blocks = []
    for b, r in enumerate(rows):
        pairs = [(mix_hbm.at[b], mix_ref.at[b]), (mown_hbm.at[r, :], mown_ref.at[r, :]), (cot_hbm.at[r, :], cot_ref.at[r, :])]
        blocks.append(launch(pairs, in_sem, 3 + 3 * b))
    hub_load = pltpu.make_async_copy(at_hbm.at[: hub_ref.shape[0], :], hub_ref, in_sem.at[3 + 3 * steps])

    @pl.when(core_ref[0] != 0)
    def _():
        hub_load.start()

    for copy in early:
        copy.wait()
    pre_ref[...] = mm(f_ref[...], w_ref[:width, :])
    for copy in loads:
        copy.wait()
    w2 = w_ref[width:, :]
    stores = []
    for b, r in enumerate(rows):
        for copy in blocks[b]:
            copy.wait()
        mean = ((mm_first(mix_ref[b], recv_ref[...]) + mown_ref[r, :]) / DEG).astype(BF)
        mean_ref[r, :] = mean
        pre = pre_ref[r, :] + mm(mean, w2)
        sig = jax.nn.sigmoid(pre)
        act_ref[r, :] = (pre * sig).astype(BF)
        delta = (cot_ref[r, :].astype(F32) * sig * (1.0 + pre * (1.0 - sig))).astype(BF)
        delta_ref[r, :] = delta
        gm_ref[r, :] = (mm_last(delta, w2) / DEG).astype(BF)
        stores += launch(
            [(act_ref.at[r, :], act_hbm.at[r, :])]
            + [
                (x.at[r, :], trio_hbm.at[i * nodes + r.start : i * nodes + r.stop, :])
                for i, x in enumerate((gm_ref, delta_ref, mean_ref))
            ],
            out_sem, 4 * b,
        )

    half = width
    tops = [slice(0, half), slice(half, 2 * half)]

    @pl.when(core_ref[0] == 0)
    def _():
        for i, (r, x) in enumerate(zip(tops, (f_ref, mean_ref))):
            give_ref[r, :] = mm_first(x[...], delta_ref[...]).astype(BF)
            pltpu.make_async_copy(give_ref.at[r, :], give_hbm.at[r, :], out_sem.at[4 * steps + i]).start()

    @pl.when(core_ref[0] != 0)
    def _():
        hub_load.wait()
        for i, r in enumerate(tops):
            give_ref[r, :] = mm(hub_ref[r, :], gm_ref[...]).astype(BF)
            pltpu.make_async_copy(give_ref.at[r, :], give_hbm.at[r, :], out_sem.at[4 * steps + i]).start()

    for i, r in enumerate(tops):
        pltpu.make_async_copy(give_ref.at[r, :], give_hbm.at[r, :], out_sem.at[4 * steps + i]).wait()
    for copy in stores:
        copy.wait()


def listed_kernel(core_ref, trio_hbm, hub_hbm, own_at_hbm, at_ref, w_ref, out_ref, own_ref, gm_ref, delta_ref, mean_ref, hub_ref, own_at_ref, sems):
    nodes = gm_ref.shape[0]
    parts_of = [trio_hbm.at[i * nodes : (i + 1) * nodes, :] for i in range(3)]
    first, second = launch([(parts_of[0], gm_ref), (parts_of[1], delta_ref)], sems)
    (third,) = launch([(own_at_hbm.at[:nodes, :], own_at_ref)], sems, 4)
    hub_load = pltpu.make_async_copy(hub_hbm.at[: hub_ref.shape[0], :], hub_ref, sems.at[2])
    mean_load = pltpu.make_async_copy(parts_of[2], mean_ref, sems.at[3])
    even = core_ref[0] == 0
    pl.when(even)(hub_load.start)
    pl.when(jnp.logical_not(even))(mean_load.start)
    first.wait()
    out_ref[...] = mm(at_ref[...], gm_ref[...]).astype(BF)
    width = own_ref.shape[1]
    third.wait()
    own = mm(own_at_ref[...], gm_ref[...])
    second.wait()
    own_ref[...] = own + mm_last(delta_ref[...], w_ref[:width, :])
    pl.when(even)(hub_load.wait)
    pl.when(jnp.logical_not(even))(mean_load.wait)


def pack_kernel(core_ref, listed_ref, gm_ref, delta_ref, mean_ref, hub_ref, f_ref, got_ref, out_ref):
    parts, _, width = out_ref.shape
    step = 32
    rows = [slice(b * step * 8, (b + 1) * step * 8) for b in range(parts // step)]

    def fill(own):
        for b, r in enumerate(rows):
            total = own(r) + got_ref[r, :].astype(F32)
            listed = listed_ref[r, :].astype(F32)
            both = jnp.concatenate([listed.reshape(step, 8, width), total.reshape(step, 8, width)], axis=1)
            out_ref[b * step : (b + 1) * step] = both.astype(BF)

    def weight_rows(r):
        x_ref = f_ref if r.start < width else mean_ref
        first = r.start % width
        return mm_first(x_ref[:, first : first + step * 8], delta_ref[...])

    @pl.when(core_ref[0] == 0)
    def _():
        fill(lambda r: mm(hub_ref[r, :], gm_ref[...]))

    @pl.when(core_ref[0] != 0)
    def _():
        fill(weight_rows)


def last_kernel(st_ref, back_ref, own_ref, hub_ref, out_hbm, weight_ref, list_ref, out_ref, sems):
    nodes, width = out_ref.shape
    step = 256
    hub_sum = jnp.zeros(weight_ref.shape, F32)
    weight_sum = jnp.zeros(weight_ref.shape, F32)
    for q in range(0, back_ref.shape[0] // 16, 2):
        even = back_ref[q * 16 : (q + 1) * 16, :].astype(F32)
        odd = back_ref[(q + 1) * 16 : (q + 2) * 16, :].astype(F32)
        hub_sum = hub_sum + even[8:, :]
        weight_sum = weight_sum + odd[8:, :]
        list_ref[q * 8 : (q + 2) * 8, :] = jnp.concatenate([even[:8, :], odd[:8, :]], axis=0).astype(BF)
    weight_ref[...] = weight_sum
    high = hub_sum.astype(BF)
    low = (hub_sum - high.astype(F32)).astype(BF)
    hub_rows = jnp.concatenate([high, low], axis=0)
    hubs = jnp.concatenate([hub_ref[...], hub_ref[...]], axis=1)
    stores = []
    for b in range(nodes // step):
        r = slice(b * step, (b + 1) * step)
        hot = (iota((step, hubs.shape[1]), 0) + b * step == hubs).astype(F32).astype(BF)
        out_ref[r, :] = (own_ref[r, :] + mm(hot, hub_rows) + mm(st_ref[r, :], list_ref[...])).astype(BF)
        stores += launch([(out_ref.at[r, :], out_hbm.at[r, :])], sems, b)
    for copy in stores:
        copy.wait()


def call(kernel, ins, outs, scratch=(), flops=0, read=0, mib=60, in_specs=None, out_specs=None):
    return pl.pallas_call(
        kernel,
        out_shape=[jax.ShapeDtypeStruct(s, d) for s, d in outs],
        in_specs=in_specs or [HB] * len(ins),
        out_specs=out_specs or [HB] * len(outs),
        scratch_shapes=[pltpu.VMEM(*x) if isinstance(x, tuple) else x for x in scratch],
        compiler_params=pltpu.CompilerParams(vmem_limit_bytes=mib * MIB),
        cost_estimate=pl.CostEstimate(flops=flops, bytes_accessed=read, transcendentals=0),
    )(*ins)


def local(features, weights, cotangent, neighbours, send_rows, send_count, hub_local):
    nodes, width = features.shape
    parts = lax.axis_size(AXES)
    halo = parts * 8
    core = (lax.axis_index("col") % 2).astype(jnp.int32).reshape(1)
    sems = lambda n: pltpu.SemaphoreType.DMA((n,))
    wide, half = ((nodes, width), F32), ((nodes, width), BF)
    packed = ((parts, 16, width), BF)

    (pay,) = call(
        send_kernel,
        [features, send_rows[0].T, send_count, hub_local],
        [packed],
        [half, ((8, parts), jnp.int32), ((1, parts), jnp.int32), ((1, 8), jnp.int32), ((parts, 8), F32), packed, sems(4), sems(parts // 32)],
        flops=2 * nodes * halo * width, read=3 * MIB,
    )
    recv = lax.all_to_all(pay, AXES, split_axis=0, concat_axis=0, tiled=True).reshape(2 * halo, width)

    live = iota((parts, 8), 1) < send_count[0][:, None]
    slot = jnp.where(live, send_rows[0], -1).reshape(1, halo)
    square = ((nodes, nodes), BF)
    hot = [square, ((halo, nodes), BF), ((halo, nodes), BF), ((2, 2 * halo, nodes // 2), BF), ((nodes, halo), BF), wide]
    outs = [((BIG * nodes, nodes), BF), hot[1], ((BIG * halo, nodes), BF)] + hot[3:]
    at_own, at_halo, at, mix, st, mean_own = call(
        hot_kernel, [neighbours.T, slot, features], outs, hot + [sems(6)],
        flops=14 * 10**9, read=20 * MIB, mib=63, in_specs=[VM] * 3,
    )
    both = ((2 * width, width), BF)
    mid = [half, half, half, half, both]
    act, trio, give = call(
        mid_kernel,
        [core, recv, mix, at, mean_own, weights, features, cotangent],
        [half, ((2 * BIG * nodes, width), BF), both],
        [((2 * halo, width), BF), ((2, 2 * halo, nodes // 2), BF), ((halo, nodes), BF), wide, both, half, half, wide]
        + mid + [sems(16), sems(18)],
        flops=6 * 10**9, read=16 * MIB, in_specs=[SM] + [HB] * 7,
    )
    got = lax.ppermute(give, AXES, [(i, i ^ 1) for i in range(parts)])
    listed, own, gm, delta, mean, hub_counts = call(
        listed_kernel, [core, trio, at, at_own, at_halo, weights], [half, wide, half, half, half, ((halo, nodes), BF)], [square, sems(5)],
        flops=3 * 10**9, read=8 * MIB, mib=24, in_specs=[SM, HB, HB, HB, VM, VM], out_specs=[VM] * 6,
    )
    (pay_back,) = call(
        pack_kernel, [core, listed, gm, delta, mean, hub_counts, features, got], [packed],
        flops=2 * 10**9, read=6 * MIB, mib=24, in_specs=[SM] + [VM] * 7, out_specs=[VM],
    )
    back = lax.all_to_all(pay_back, AXES, split_axis=0, concat_axis=0, tiled=True).reshape(2 * halo, width)
    grad, grad_weights = call(
        last_kernel, [st, back, own, hub_local], [half, ((8, width), F32)],
        [((halo, width), BF), half, sems(4)],
        flops=4 * 10**9, read=10 * MIB, mib=24, in_specs=[VM] * 4, out_specs=[HB, VM],
    )
    return act, grad, grad_weights


def solution(mesh):
    both = P(AXES, None)
    placed = (both, P(), both, both, P(AXES, None, None), both, both)
    return jax.shard_map(local, mesh=mesh, in_specs=placed, out_specs=(both, both, both), check_vma=False)
```

```python
import jax
import jax.numpy as jnp
from jax import lax
from jax.experimental import pallas as pl
from jax.experimental.pallas import tpu as pltpu
from jax.sharding import PartitionSpec as P

BF = jnp.bfloat16
F32 = jnp.float32
DEG = 8
BIG = 12
AXES = ("row", "col")
VM = pl.BlockSpec(memory_space=pltpu.VMEM)
SM = pl.BlockSpec(memory_space=pltpu.SMEM)
HB = pl.BlockSpec(memory_space=pltpu.HBM)
MIB = 1024 * 1024


def iota(shape, dim):
    return lax.broadcasted_iota(jnp.int32, shape, dim)


def mm(a, b):
    return jnp.dot(a, b, preferred_element_type=F32)


def mm_last(a, b):
    return lax.dot_general(a, b, (((1,), (1,)), ((), ())), preferred_element_type=F32)


def mm_first(a, b):
    return lax.dot_general(a, b, (((0,), (0,)), ((), ())), preferred_element_type=F32)


def send_kernel(f_hbm, rows_hbm, count_hbm, hub_hbm, out_hbm, f_ref, rows_ref, count_ref, hub_ref, idx_ref, out_ref, sem, out_sem):
    loads = [
        pltpu.make_async_copy(src, dst, sem.at[i])
        for i, (src, dst) in enumerate(
            ((f_hbm, f_ref), (rows_hbm, rows_ref), (count_hbm, count_ref), (hub_hbm, hub_ref))
        )
    ]
    for copy in loads:
        copy.start()
    for copy in loads[1:]:
        copy.wait()
    parts = rows_ref.shape[1]
    nodes = f_ref.shape[0]
    live = iota((8, parts), 0) < count_ref[...]
    idx = jnp.where(live, rows_ref[...], -1).astype(F32)
    idx_ref[...] = idx.T
    hub = jnp.broadcast_to(hub_ref[...], (8, 8))
    hub_col = jnp.sum(jnp.where(iota((8, 8), 0) == iota((8, 8), 1), hub, 0), axis=1, keepdims=True)
    hub_hot = (iota((8, nodes), 1) == hub_col).astype(F32).astype(BF)
    loads[0].wait()
    hub_rows = mm(hub_hot, f_ref[...])
    step = 32
    stores = []
    for b in range(parts // step):
        blk = idx_ref[b * step : (b + 1) * step, :]
        wide = jnp.broadcast_to(blk[:, None, :], (step, 8, 8)).reshape(step * 8, 8)
        pick = iota((step * 8, 8), 0) % 8 == iota((step * 8, 8), 1)
        col = jnp.sum(jnp.where(pick, wide, 0.0), axis=1, keepdims=True).astype(jnp.int32)
        hot = (iota((step * 8, nodes), 1) == col).astype(F32).astype(BF)
        listed = mm(hot, f_ref[...]).reshape(step, 8, -1)
        both = jnp.concatenate(
            [listed, jnp.broadcast_to(hub_rows[None], (step, 8, hub_rows.shape[1]))], axis=1
        )
        at = slice(b * step, (b + 1) * step)
        out_ref[at] = both.astype(BF)
        stores.append(pltpu.make_async_copy(out_ref.at[at], out_hbm.at[at], out_sem.at[b]))
        stores[-1].start()
    for copy in stores:
        copy.wait()


def unique(t):
    keep, count = [], []
    for k in range(DEG):
        row = t[k : k + 1]
        total = jnp.zeros_like(row)
        seen = None
        for j in range(DEG):
            same = t[j : j + 1] == row
            total = total + jnp.where(same, 1.0, 0.0)
            if j < k:
                seen = same if seen is None else seen | same
        keep.append(row if seen is None else jnp.where(seen, -1.0, row))
        count.append(total)
    return jnp.concatenate(keep, axis=0), jnp.concatenate(count, axis=0)


def count_matrix(u, m, outs):
    span = 256
    first = 0
    for out_ref in outs:
        lanes = out_ref.shape[1]
        at = slice(first, first + lanes)
        first += lanes
        counts = [jnp.broadcast_to(m[k : k + 1, at], (16, lanes)).astype(BF) for k in range(DEG)]
        base = iota((16, lanes), 0).astype(F32).astype(BF)

        @pl.loop(0, out_ref.shape[0] // span)
        def _(b):
            near = jnp.clip(u[:, at] - (b * span).astype(F32), -1.0, float(span))
            names = [jnp.broadcast_to(near[k : k + 1], (16, lanes)).astype(BF) for k in range(DEG)]
            for h in range(0, span, 16):
                it = base + BF(h)
                acc = jnp.zeros((16, lanes), BF)
                for k in range(DEG):
                    acc = jnp.where(it == names[k], counts[k], acc)
                out_ref[pl.ds(pl.multiple_of(b * span + h, 16), 16), :] = acc


def launch(pairs, sems, first=0):
    copies = [pltpu.make_async_copy(src, dst, sems.at[first + i]) for i, (src, dst) in enumerate(pairs)]
    for copy in copies:
        copy.start()
    return copies


def hot_kernel(nb_ref, slot_ref, f_ref, own_hbm, listed_hbm, hub_hbm, mix_hbm, st_hbm, mown_hbm,
               own_ref, listed_ref, hub_ref, mix_ref, st_ref, mown_ref, sems):
    nodes = f_ref.shape[0]
    halo = hub_ref.shape[0]
    half = nodes // 2
    cols = [slice(0, half), slice(half, nodes)]
    u, m = unique(nb_ref[...].astype(F32))
    w = u.astype(jnp.int32) - nodes
    is_hub = w >= halo
    v = jnp.where(is_hub, w - halo, w)
    v = (v // 8) * 16 + v % 8 + jnp.where(is_hub, 8, 0)
    count_matrix(jnp.where(w < 0, -1, v).astype(F32), m, [mix_ref.at[c] for c in range(mix_ref.shape[0])])
    copies = launch([(mix_ref, mix_hbm)], sems, 0)
    count_matrix(u, m, [own_ref.at[:, c] for c in cols])
    mown_ref[...] = mm_first(own_ref[...], f_ref[...])
    copies += launch([(own_ref, own_hbm), (mown_ref, mown_hbm)], sems, 1)
    count_matrix(u - nodes, m, [listed_ref.at[:, c] for c in cols])
    count_matrix(u - (nodes + halo), m, [hub_ref.at[:, c] for c in cols])
    copies += launch([(listed_ref, listed_hbm), (hub_ref, hub_hbm.at[:halo, :])], sems, 3)
    slot = slot_ref[...]

    @pl.loop(0, nodes // 16)
    def _(b):
        it = iota((16, slot.shape[1]), 0) + b * 16
        st_ref[pl.ds(pl.multiple_of(b * 16, 16), 16), :] = (it == slot).astype(F32).astype(BF)

    copies += launch([(st_ref, st_hbm)], sems, 5)
    for copy in copies:
        copy.wait()


def mid_kernel(core_ref, recv_hbm, mix_hbm, at_hbm, mown_hbm, w_hbm, f_hbm, cot_hbm,
               act_hbm, trio_hbm, give_hbm,
               recv_ref, mix_ref, hub_ref, mown_ref, w_ref, f_ref, cot_ref, pre_ref,
               act_ref, delta_ref, gm_ref, mean_ref, give_ref, in_sem, out_sem):
    nodes, width = delta_ref.shape
    step = 512
    steps = nodes // step
    rows = [slice(b * step, (b + 1) * step) for b in range(steps)]
    early = launch([(w_hbm, w_ref), (f_hbm, f_ref)], in_sem, 0)
    loads = launch([(recv_hbm, recv_ref)], in_sem, 2)
    blocks = []
    for b, r in enumerate(rows):
        pairs = [(mix_hbm.at[b], mix_ref.at[b]), (mown_hbm.at[r, :], mown_ref.at[r, :]), (cot_hbm.at[r, :], cot_ref.at[r, :])]
        blocks.append(launch(pairs, in_sem, 3 + 3 * b))
    hub_load = pltpu.make_async_copy(at_hbm.at[: hub_ref.shape[0], :], hub_ref, in_sem.at[3 + 3 * steps])

    @pl.when(core_ref[0] != 0)
    def _():
        hub_load.start()

    for copy in early:
        copy.wait()
    pre_ref[...] = mm(f_ref[...], w_ref[:width, :])
    for copy in loads:
        copy.wait()
    w2 = w_ref[width:, :]
    stores = []
    for b, r in enumerate(rows):
        for copy in blocks[b]:
            copy.wait()
        mean = ((mm_first(mix_ref[b], recv_ref[...]) + mown_ref[r, :]) / DEG).astype(BF)
        mean_ref[r, :] = mean
        pre = pre_ref[r, :] + mm(mean, w2)
        sig = jax.nn.sigmoid(pre)
        act_ref[r, :] = (pre * sig).astype(BF)
        delta = (cot_ref[r, :].astype(F32) * sig * (1.0 + pre * (1.0 - sig))).astype(BF)
        delta_ref[r, :] = delta
        gm_ref[r, :] = (mm_last(delta, w2) / DEG).astype(BF)
        stores += launch(
            [(act_ref.at[r, :], act_hbm.at[r, :])]
            + [
                (x.at[r, :], trio_hbm.at[i * nodes + r.start : i * nodes + r.stop, :])
                for i, x in enumerate((gm_ref, delta_ref, mean_ref))
            ],
            out_sem, 4 * b,
        )

    half = width
    tops = [slice(0, half), slice(half, 2 * half)]

    @pl.when(core_ref[0] == 0)
    def _():
        for i, (r, x) in enumerate(zip(tops, (f_ref, mean_ref))):
            give_ref[r, :] = mm_first(x[...], delta_ref[...]).astype(BF)
            pltpu.make_async_copy(give_ref.at[r, :], give_hbm.at[r, :], out_sem.at[4 * steps + i]).start()

    @pl.when(core_ref[0] != 0)
    def _():
        hub_load.wait()
        for i, r in enumerate(tops):
            give_ref[r, :] = mm(hub_ref[r, :], gm_ref[...]).astype(BF)
            pltpu.make_async_copy(give_ref.at[r, :], give_hbm.at[r, :], out_sem.at[4 * steps + i]).start()

    for i, r in enumerate(tops):
        pltpu.make_async_copy(give_ref.at[r, :], give_hbm.at[r, :], out_sem.at[4 * steps + i]).wait()
    for copy in stores:
        copy.wait()


def listed_kernel(core_ref, trio_hbm, hub_hbm, at_ref, w_ref, out_ref, own_ref, gm_ref, delta_ref, mean_ref, hub_ref, sems):
    nodes = gm_ref.shape[0]
    parts_of = [trio_hbm.at[i * nodes : (i + 1) * nodes, :] for i in range(3)]
    first, second = launch([(parts_of[0], gm_ref), (parts_of[1], delta_ref)], sems)
    hub_load = pltpu.make_async_copy(hub_hbm.at[: hub_ref.shape[0], :], hub_ref, sems.at[2])
    mean_load = pltpu.make_async_copy(parts_of[2], mean_ref, sems.at[3])
    even = core_ref[0] == 0
    pl.when(even)(hub_load.start)
    pl.when(jnp.logical_not(even))(mean_load.start)
    first.wait()
    out_ref[...] = mm(at_ref[...], gm_ref[...]).astype(BF)
    second.wait()
    own_ref[...] = mm_last(delta_ref[...], w_ref[: own_ref.shape[1], :])
    pl.when(even)(hub_load.wait)
    pl.when(jnp.logical_not(even))(mean_load.wait)


def pack_kernel(core_ref, listed_ref, gm_ref, delta_ref, mean_ref, hub_ref, f_ref, got_ref, out_ref):
    parts, _, width = out_ref.shape
    step = 32
    rows = [slice(b * step * 8, (b + 1) * step * 8) for b in range(parts // step)]

    def fill(own):
        for b, r in enumerate(rows):
            total = own(r) + got_ref[r, :].astype(F32)
            listed = listed_ref[r, :].astype(F32)
            both = jnp.concatenate([listed.reshape(step, 8, width), total.reshape(step, 8, width)], axis=1)
            out_ref[b * step : (b + 1) * step] = both.astype(BF)

    def weight_rows(r):
        x_ref = f_ref if r.start < width else mean_ref
        first = r.start % width
        return mm_first(x_ref[:, first : first + step * 8], delta_ref[...])

    @pl.when(core_ref[0] == 0)
    def _():
        fill(lambda r: mm(hub_ref[r, :], gm_ref[...]))

    @pl.when(core_ref[0] != 0)
    def _():
        fill(weight_rows)


def last_kernel(st_ref, back_ref, at_ref, gm_ref, own_ref, hub_ref, out_hbm, weight_ref, list_ref, out_ref, sems):
    nodes, width = out_ref.shape
    step = 256
    hub_sum = jnp.zeros(weight_ref.shape, F32)
    weight_sum = jnp.zeros(weight_ref.shape, F32)
    for q in range(0, back_ref.shape[0] // 16, 2):
        even = back_ref[q * 16 : (q + 1) * 16, :].astype(F32)
        odd = back_ref[(q + 1) * 16 : (q + 2) * 16, :].astype(F32)
        hub_sum = hub_sum + even[8:, :]
        weight_sum = weight_sum + odd[8:, :]
        list_ref[q * 8 : (q + 2) * 8, :] = jnp.concatenate([even[:8, :], odd[:8, :]], axis=0).astype(BF)
    weight_ref[...] = weight_sum
    high = hub_sum.astype(BF)
    low = (hub_sum - high.astype(F32)).astype(BF)
    hub_rows = jnp.concatenate([high, low], axis=0)
    hubs = jnp.concatenate([hub_ref[...], hub_ref[...]], axis=1)
    stores = []
    for b in range(nodes // step):
        r = slice(b * step, (b + 1) * step)
        own = mm(at_ref[r, :], gm_ref[...]) + own_ref[r, :]
        hot = (iota((step, hubs.shape[1]), 0) + b * step == hubs).astype(F32).astype(BF)
        out_ref[r, :] = (own + mm(hot, hub_rows) + mm(st_ref[r, :], list_ref[...])).astype(BF)
        stores += launch([(out_ref.at[r, :], out_hbm.at[r, :])], sems, b)
    for copy in stores:
        copy.wait()


def call(kernel, ins, outs, scratch=(), flops=0, read=0, mib=60, in_specs=None, out_specs=None):
    return pl.pallas_call(
        kernel,
        out_shape=[jax.ShapeDtypeStruct(s, d) for s, d in outs],
        in_specs=in_specs or [HB] * len(ins),
        out_specs=out_specs or [HB] * len(outs),
        scratch_shapes=[pltpu.VMEM(*x) if isinstance(x, tuple) else x for x in scratch],
        compiler_params=pltpu.CompilerParams(vmem_limit_bytes=mib * MIB),
        cost_estimate=pl.CostEstimate(flops=flops, bytes_accessed=read, transcendentals=0),
    )(*ins)


def local(features, weights, cotangent, neighbours, send_rows, send_count, hub_local):
    nodes, width = features.shape
    parts = lax.axis_size(AXES)
    halo = parts * 8
    core = (lax.axis_index("col") % 2).astype(jnp.int32).reshape(1)
    sems = lambda n: pltpu.SemaphoreType.DMA((n,))
    wide, half = ((nodes, width), F32), ((nodes, width), BF)
    packed = ((parts, 16, width), BF)

    (pay,) = call(
        send_kernel,
        [features, send_rows[0].T, send_count, hub_local],
        [packed],
        [half, ((8, parts), jnp.int32), ((1, parts), jnp.int32), ((1, 8), jnp.int32), ((parts, 8), F32), packed, sems(4), sems(parts // 32)],
        flops=2 * nodes * halo * width, read=3 * MIB,
    )
    recv = lax.all_to_all(pay, AXES, split_axis=0, concat_axis=0, tiled=True).reshape(2 * halo, width)

    live = iota((parts, 8), 1) < send_count[0][:, None]
    slot = jnp.where(live, send_rows[0], -1).reshape(1, halo)
    square = ((nodes, nodes), BF)
    hot = [square, ((halo, nodes), BF), ((halo, nodes), BF), ((2, 2 * halo, nodes // 2), BF), ((nodes, halo), BF), wide]
    outs = hot[:2] + [((BIG * halo, nodes), BF)] + hot[3:]
    at_own, at_halo, at, mix, st, mean_own = call(
        hot_kernel, [neighbours.T, slot, features], outs, hot + [sems(6)],
        flops=14 * 10**9, read=20 * MIB, mib=63, in_specs=[VM] * 3,
    )
    both = ((2 * width, width), BF)
    mid = [half, half, half, half, both]
    act, trio, give = call(
        mid_kernel,
        [core, recv, mix, at, mean_own, weights, features, cotangent],
        [half, ((2 * BIG * nodes, width), BF), both],
        [((2 * halo, width), BF), ((2, 2 * halo, nodes // 2), BF), ((halo, nodes), BF), wide, both, half, half, wide]
        + mid + [sems(16), sems(18)],
        flops=6 * 10**9, read=16 * MIB, in_specs=[SM] + [HB] * 7,
    )
    got = lax.ppermute(give, AXES, [(i, i ^ 1) for i in range(parts)])
    listed, own, gm, delta, mean, hub_counts = call(
        listed_kernel, [core, trio, at, at_halo, weights], [half, wide, half, half, half, ((halo, nodes), BF)], [sems(4)],
        flops=10**9, read=4 * MIB, mib=24, in_specs=[SM, HB, HB, VM, VM], out_specs=[VM] * 6,
    )
    (pay_back,) = call(
        pack_kernel, [core, listed, gm, delta, mean, hub_counts, features, got], [packed],
        flops=2 * 10**9, read=6 * MIB, mib=24, in_specs=[SM] + [VM] * 7, out_specs=[VM],
    )
    back = lax.all_to_all(pay_back, AXES, split_axis=0, concat_axis=0, tiled=True).reshape(2 * halo, width)
    grad, grad_weights = call(
        last_kernel, [st, back, at_own, gm, own, hub_local], [half, ((8, width), F32)],
        [((halo, width), BF), half, sems(4)],
        flops=4 * 10**9, read=10 * MIB, mib=24, in_specs=[VM] * 6, out_specs=[HB, VM],
    )
    return act, grad, grad_weights


def solution(mesh):
    both = P(AXES, None)
    placed = (both, P(), both, both, P(AXES, None, None), both, both)
    return jax.shard_map(local, mesh=mesh, in_specs=placed, out_specs=(both, both, both), check_vma=False)
```
